512 devices in a mesh: slab: 128 (over x, z, core), depth: 4 (over y).
Axes of the slice: x: 4, y: 4, z: 16, core: 2. Of those that a mesh axis runs over, the one named last changes fastest.
Arguments:
- right_side: float32 [3, 8, 128, 32, 256], P(None, None, 'slab', 'depth'), may hold values from -4 to 9
- smoother: float32 [3, 128, 32, 256], P(None, 'slab', 'depth'), may hold values from 0.1 to 1
- material: int32 [128, 32, 256], P('slab', 'depth'), may hold values from 0 to 15
- moduli: float32 [16], replicated, may hold values from 0.25 to 4
- element_matrix: float32 [24, 24], replicated, may hold values from -0.15 to 3, as said below
- coarse_inverse: float32 [384, 384], replicated, may hold values from -0.2 to 1.2, as said below
- surface_map: int32 [128, 256], P('slab'), may hold values from 0 to 32767, as said below
- line_of_sight: float32 [3, 128, 256], P(None, 'slab'), may hold values from -3 to 3
Outputs:
- residual: float32 [3, 8, 128, 32, 256], P(None, None, 'slab', 'depth')
- pixels: float32 [8, 32768], P('depth', 'slab')
The draws below stay inside these ranges and needn't reach their ends.
Inputs may be any that keep to these rules, and one draw needn't show every extreme that they name: `element_matrix`: symmetric. `coarse_inverse`: symmetric. `surface_map`: pixel p lies in tile p // 256. At most 4 surface nodes of one slab block lie in one tile, and some tile holds exactly 4 surface nodes of every slab block.
All inputs are finite; a program needn't handle non-finite values.
Results may differ from the reference program's by a relative error of at most 0.0003.
Values sent between devices are 32-bit elements; how exact they have to be, the bound alone decides.
A program may use at most 64 MiB of HBM per device.

```python
import math
import jax
import jax.numpy as jnp
from jax import lax

SRC = 8
NMAT = 16
CX = 1
NY = 256
PIX = 256
NX = 128
NZ = 32
PIXELS = 32768
N_SLAB = 128


def draw_right_side(key, part):
    first_key, second_key = jax.random.split(jax.random.fold_in(key, 11))
    n_blocks = NX // CX
    blocks = jnp.arange(n_blocks, dtype=jnp.float32)
    rising = 1.0 + 2.0 * blocks / max(n_blocks - 1, 1)
    roughness = jax.random.truncated_normal(first_key, -4.0, 4.0, (3, SRC, NX, NZ, NY), jnp.float32)
    amplitude = jax.random.uniform(second_key, (3, SRC, n_blocks), jnp.float32, 0.5, 1.5)
    smooth_part = jnp.repeat(amplitude * rising, CX, axis=2)
    return roughness + smooth_part[:, :, :, None, None]


def draw_element_matrix(key, part):
    first_key, second_key = jax.random.split(jax.random.fold_in(key, 23))
    normal_part = jax.random.truncated_normal(first_key, -4.0, 4.0, (24, 24), jnp.float32) * 0.02
    margin = jax.random.uniform(second_key, (24,), jnp.float32, 0.05, 0.15)
    off_diag = 0.5 * (normal_part + normal_part.T) * (1.0 - jnp.eye(24, dtype=jnp.float32))
    diagonal_part = jnp.sum(jnp.abs(off_diag), axis=1) + margin
    return off_diag + jnp.diag(diagonal_part)


def draw_coarse_inverse(key, part):
    size_kc = 3 * (NX // CX)
    normal_part = jax.random.truncated_normal(jax.random.fold_in(key, 37), -4.0, 4.0, (size_kc, size_kc), jnp.float32)
    normal_part = normal_part * (0.2 / size_kc ** 0.5)
    return jnp.eye(size_kc, dtype=jnp.float32) + 0.5 * (normal_part + normal_part.T)


def draw_surface_map(key, part):
    n_blocks = NX // CX
    node_count = CX * NY
    capacity = 2 * node_count // n_blocks
    pair_count = n_blocks // 2
    full_pair = jax.random.randint(jax.random.fold_in(key, 7), (), 0, pair_count)

    def one_block(block_id):
        block_key = jax.random.fold_in(key, block_id + 100)
        first_key, second_key, third_key = jax.random.split(block_key, 3)
        counts = jax.random.randint(first_key, (pair_count,), 0, capacity + 1)
        counts = jnp.where(jnp.arange(pair_count, dtype=jnp.int32) == full_pair, capacity, counts)
        positions = jnp.arange(node_count, dtype=jnp.int32)
        pair_of = positions // capacity
        within = positions % capacity
        tile_owner = 2 * pair_of + (within >= counts[pair_of]).astype(jnp.int32)
        shuffle = jax.random.permutation(second_key, node_count)
        tile_owner = tile_owner[shuffle]
        pixel_local = jax.random.randint(third_key, (node_count,), 0, PIX)
        return (tile_owner * PIX + pixel_local).astype(jnp.int32)
    tables = jax.vmap(one_block)(jnp.arange(n_blocks, dtype=jnp.int32))
    return tables.reshape(NX, NY)


def set_ends(values, own_key, low, top_value):
    shape = values.shape
    place = [jax.random.randint(jax.random.fold_in(own_key, axis), (), 0, shape[axis]) for axis in range(len(shape))]
    values = values.at[tuple(place)].set(low)
    longest = shape.index(max(shape))
    place[longest] = (place[longest] + 1) % shape[longest]
    return values.at[tuple(place)].set(top_value)


def steps_of(own_key, dims, cuts, smallest, top_value):
    factor_of, own = 1.0, jax.random.fold_in(own_key, 6)
    for position, blocks in cuts:
        heights = jnp.exp(jax.random.uniform(jax.random.fold_in(own, position), (blocks,), jnp.float32, smallest / len(cuts), top_value / len(cuts)))
        factor_of = factor_of * jnp.repeat(heights, dims[position] // blocks).reshape([-1 if axis == position else 1 for axis in range(len(dims))])
    return factor_of


def centred(own_key, dims, scale, limit, shards=(), kind=jnp.bfloat16):
    level = steps_of(own_key, dims, shards, -0.22, 0.18) if shards else 1.0
    array = jax.random.normal(own_key, dims, jnp.float32) * scale * level
    return jnp.minimum(jnp.maximum(array, -limit), limit).astype(kind)


def setup_inputs(seed: int = 0) -> dict:
    splits = jax.random.split(jax.random.key(seed), 9)
    right_side = draw_right_side(jax.random.fold_in(splits[8], 71), 0)
    smoother = jnp.clip(jnp.exp(math.log(1.0) - 2.3025851 * jax.random.uniform(splits[1], (3, NX, NZ, NY), jnp.float32) ** steps_of(splits[1], (3, NX, NZ, NY), ((1, 128), (2, 4)), -0.2, 0.2)), 0.1, 1.0)
    material = set_ends(jax.random.randint(splits[2], (NX, NZ, NY), 0, NMAT), jax.random.fold_in(splits[2], 1), 0, NMAT - 1).astype(jnp.int32)
    moduli = jnp.clip(jnp.exp(jax.random.uniform(splits[3], (NMAT,), jnp.float32, math.log(0.25), math.log(4.0))), 0.25, 4.0)
    element_matrix = draw_element_matrix(jax.random.fold_in(splits[8], 71), 0)
    coarse_inverse = draw_coarse_inverse(jax.random.fold_in(splits[8], 71), 0)
    surface_map = draw_surface_map(jax.random.fold_in(splits[8], 71), 0)
    line_of_sight = centred(splits[7], (3, NX, NY), 0.6, 3.0, ((1, 128),), jnp.float32)
    return dict(right_side=right_side, smoother=smoother, material=material, moduli=moduli, element_matrix=element_matrix, coarse_inverse=coarse_inverse, surface_map=surface_map, line_of_sight=line_of_sight)


def stiffness(padded_field, padded_moduli, element_matrix):
    sources = padded_field.shape[1]
    span_x = padded_field.shape[2] - 1
    span_z = padded_field.shape[3] - 1
    span_y = padded_moduli.shape[2]
    corners = []
    for corner in range(8):
        along_x, along_z, along_y = corner // 4, (corner // 2) % 2, corner % 2
        corners.append(padded_field[:, :, along_x:along_x + span_x, along_z:along_z + span_z, along_y:along_y + span_y])
    stacked = jnp.stack(corners, 0).reshape(24, -1)
    forces = jnp.dot(element_matrix, stacked, precision=lax.Precision.HIGHEST, preferred_element_type=jnp.float32)
    forces = forces.reshape(8, 3, sources, span_x, span_z, span_y) * padded_moduli[1:, 1:, :]
    forces = jnp.pad(forces, ((0, 0), (0, 0), (0, 0), (0, 0), (0, 0), (0, 1)))
    summed = jnp.zeros((3, sources, span_x - 1, span_z - 1, span_y), jnp.float32)
    for corner in range(8):
        along_x, along_z, along_y = corner // 4, (corner // 2) % 2, corner % 2
        summed = summed + forces[corner, :, :, 1 - along_x:1 - along_x + span_x - 1, 1 - along_z:1 - along_z + span_z - 1, 1 - along_y:1 - along_y + span_y]
    return summed


def reference(right_side, smoother, material, moduli, element_matrix, coarse_inverse, surface_map, line_of_sight):
    modulus_field = moduli[material]
    block_sums = right_side.reshape(3, SRC, N_SLAB, CX * NZ * NY).sum(-1)
    coarse_mean = jnp.transpose(block_sums, (2, 0, 1)).reshape(3 * N_SLAB, SRC) / (CX * NZ * NY)
    correction = jnp.dot(coarse_inverse, coarse_mean, precision=lax.Precision.HIGHEST, preferred_element_type=jnp.float32)
    per_block = jnp.transpose(correction.reshape(N_SLAB, 3, SRC), (1, 2, 0))
    per_node = jnp.repeat(per_block, CX, axis=2)
    direction = smoother[:, None] * right_side + per_node[:, :, :, None, None]
    numerator = jnp.sum(right_side * direction, axis=(0, 2, 3, 4))
    padded = jnp.pad(direction, ((0, 0), (0, 0), (1, 1), (1, 1), (1, 0)))
    moduli_pad = jnp.pad(modulus_field, ((1, 1), (1, 1), (0, 0)))

    def block_apply(block_index):
        offset = (block_index * CX).astype(jnp.int32)
        field_blk = lax.dynamic_slice_in_dim(padded, offset, CX + 2, 2)
        moduli_blk = lax.dynamic_slice_in_dim(moduli_pad, offset, CX + 2, 0)
        return stiffness(field_blk, moduli_blk, element_matrix)

    applied = lax.map(block_apply, jnp.arange(N_SLAB, dtype=jnp.int32))
    applied = jnp.transpose(applied, (1, 2, 0, 3, 4, 5)).reshape(3, SRC, NX, NZ, NY)
    denominator = jnp.sum(direction * applied, axis=(0, 2, 3, 4))
    step_size = numerator / denominator
    residual = right_side - step_size[None, :, None, None, None] * applied
    surface = step_size[None, :, None, None] * direction[:, :, :, NZ - 1, :]
    projected = jnp.sum(line_of_sight[:, None] * surface, axis=0)
    pixels = jnp.zeros((SRC, PIXELS), jnp.float32).at[:, surface_map.reshape(-1)].add(projected.reshape(SRC, -1))
    return residual, pixels
```

```python
import jax
import jax.numpy as jnp
from jax import lax
from jax.experimental import pallas as pl
from jax.experimental.pallas import tpu as pltpu
from jax.sharding import PartitionSpec as P

F32, BF16 = jnp.float32, jnp.bfloat16
MESH = pl.DeviceIdType.MESH
HIGHEST = lax.Precision.HIGHEST
NX, NZ, NC, ND = 4, 16, 2, 4
SLABS, ROWS, NY = NX * NZ * NC, 8, 256
NODES = ROWS * ND * NY


def iota(shape, dim):
    return lax.broadcasted_iota(jnp.int32, shape, dim)


def dot(a, b):
    return jnp.dot(a, b, preferred_element_type=F32)


def dot_full(a, b):
    return jnp.dot(a, b, preferred_element_type=F32, precision=HIGHEST)


def dot_nt(a, b):
    return lax.dot_general(a, b, (((1,), (1,)), ((), ())), preferred_element_type=F32)


def split(v):
    high = v.astype(BF16)
    return high, (v - high.astype(F32)).astype(BF16)


def fsplit(v):
    high = v.astype(BF16).astype(F32)
    return high, v - high


def hot(mask):
    return jnp.where(mask, 1.0, 0.0).astype(F32)


def from_right(v):
    width = v.shape[1]
    return jnp.where(iota(v.shape, 1) == width - 1, 0.0, pltpu.roll(v, width - 1, axis=1))


def from_left(v):
    return jnp.where(iota(v.shape, 1) == 0, 0.0, pltpu.roll(v, 1, axis=1))


def to_row(columns):
    lane, sub = iota((8, 128), 1), iota((8, 128), 0)
    total = jnp.zeros((8, 128), F32)
    for q, column in enumerate(columns):
        total = jnp.where(lane == q * 8 + sub, column, total)
    return jnp.sum(total, axis=0, keepdims=True)


def pick_row(v, index):
    return jnp.sum(jnp.where(iota(v.shape, 0) == index, v, 0.0), axis=0, keepdims=True)


def kernel(
    r_ref, s_ref, mat_ref, mod_ref, e_ref, c_ref, map_ref, los_ref,
    res_ref, pix_ref,
    rt, st, hp, hz, own_mod, mod_in, mods, w, f_own, lhs_own, lhs_nb, app, g_z,
    c_perm, pj_out, pj_in, y_out, y_in, ms, r1, r2, gps,
    ly_out, ly_in, lz_out, lz_in, lx_out, lx_in,
    send, recv,
):
    s, d = lax.axis_index("slab"), lax.axis_index("depth")
    x, z, c = s // 32, (s // 2) % 16, s % 2
    g = x * 2 + c
    up, down = lax.rem(s + 1, SLABS), lax.rem(s + SLABS - 1, SLABS)
    deeper, higher = lax.rem(d + 1, ND), lax.rem(d + ND - 1, ND)

    y_peers = [(s, lax.rem(d + i, ND)) for i in range(1, ND)]
    z_ids = [lax.rem(z + i, NZ) for i in range(1, NZ)]
    z_peers = [(x * 32 + i * 2 + c, d) for i in z_ids]
    g_ids = [lax.rem(g + i, 8) for i in range(1, 8)]
    g_peers = [((i // 2) * 32 + z * 2 + i % 2, d) for i in g_ids]
    near = [(up, d), (down, d)] + [(a, b) for a in (up, down) for b in (deeper, higher)]

    barrier = pltpu.get_barrier_semaphore()
    peers = y_peers + z_peers + g_peers + near
    for peer in peers:
        pl.semaphore_signal(barrier, inc=1, device_id=peer, device_id_type=MESH)

    def copy(src, dst, index, peer):
        return pltpu.make_async_remote_copy(
            src_ref=src, dst_ref=dst, send_sem=send.at[index], recv_sem=recv.at[index],
            device_id=peer, device_id_type=MESH,
        )

    field = jnp.transpose(r_ref[...], (1, 0, 2))
    rt[...] = field
    for k in range(ROWS):
        weight = jnp.concatenate(
            [jnp.broadcast_to(s_ref[m, k : k + 1, :], (8, NY)) for m in range(3)], axis=0
        )
        st[k] = field[k] * weight
    material = mat_ref[...]
    modulus = jnp.zeros((ROWS, NY), F32)
    for i in range(16):
        modulus = jnp.where(material == i, mod_ref[i], modulus)
    own_mod[...] = modulus
    sums = jnp.sum(jnp.sum(field, axis=0), axis=1, keepdims=True)
    blocks = [sums[m * 8 : m * 8 + 8] for m in range(3)]
    row = to_row(blocks)
    y_out[...] = row
    y_in[d] = row
    shown = jnp.zeros((8, NY), F32)
    for m in range(3):
        shown = shown + los_ref[m] * st[ROWS - 1, m * 8 : m * 8 + 8, :]
    pj_out[...] = shown

    pl.semaphore_wait(barrier, len(peers))

    started = []
    for i, peer in enumerate(y_peers):
        started.append(copy(y_out, y_in.at[d], i, peer))
        started[-1].start()
    for i, peer in enumerate([(down, d), (s, higher), (down, higher)]):
        started.append(copy(own_mod, mod_in.at[i], 3 + i, peer))
        started[-1].start()

    def shows():
        return [copy(pj_out, pj_in, 6 + i, (s, i)) for i in range(ND - 1)]

    @pl.when(d == ND - 1)
    def _():
        for each in shows():
            each.start()
        pj_in[...] = shown

    sides = []
    for plane, a in ((1, s), (2, down), (0, up)):
        sides.append((st.at[0], hz.at[plane, 1], (a, higher)))
        sides.append((st.at[ROWS - 1], hz.at[plane, 0], (a, deeper)))
    for i, (src, dst, peer) in enumerate(sides):
        started.append(copy(src, dst, 9 + i, peer))
        started[-1].start()
    for i, (plane, peer) in enumerate(((1, (down, d)), (0, (up, d)))):
        started.append(copy(st, hp.at[plane], 15 + i, peer))
        started[-1].start()

    target = map_ref[...]
    tile, in_tile = target >> 8, target & 255
    tile_col = jnp.transpose(jnp.broadcast_to(tile.astype(F32), (8, NY)))[:, 0:1]
    same = (tile_col == tile.astype(F32)) & (iota((NY, NY), 0) < iota((NY, NY), 1))
    rank = jnp.sum(hot(same), axis=0, keepdims=True).astype(jnp.int32)
    tile_g = (tile >> 5) * 2 + (tile & 1)
    place_row = (tile_g >> 2) * 16 + ((tile >> 1) & 15)
    place_lane = (tile_g & 3) * 32 + rank
    row_hot = hot(iota((32, NY), 0) == place_row)

    e = e_ref[...]
    rho, eps = iota((192, 24), 0), iota((192, 24), 1)
    picked = dot_full(hot(eps == (rho % 96) // 8 + 12 * (1 - rho // 96)), e)
    eps, kap = iota((24, 192), 0), iota((24, 192), 1)
    column = 6 * (kap // 96) + (kap % 48) // 8
    wide = [dot_full(picked, hot(eps == column + 12 * a)) for a in range(2)]
    rho, kap = iota((96, 192), 0), iota((96, 192), 1)
    same_source = rho % 8 == kap % 8
    first = same_source & (kap % 96 < 48)
    parts = [wide[1][:96], wide[0][96:], wide[0][:96], wide[1][96:]]
    for i, part in enumerate(parts):
        high, low = fsplit(part)
        high = jnp.where(same_source, high, 0.0).astype(BF16)
        low = jnp.where(first, low, 0.0).astype(BF16)
        if i < 2:
            lhs_own[0, i * 96 : i * 96 + 96] = high
            lhs_own[1, i * 96 : i * 96 + 96] = low
        else:
            lhs_nb[i - 2, 0] = high
            lhs_nb[i - 2, 1] = low

    @pl.when(d != ND - 1)
    def _():
        copy(pj_out, pj_in, 6 + d, (s, d)).wait_recv()

    for i in range(3):
        copy(y_out, y_in.at[0], i, y_peers[i]).wait_recv()
    block_row = y_in[0] + y_in[1] + y_in[2] + y_in[3]
    shown = pj_in[...]
    values = [pick_row(shown, 2 * d), pick_row(shown, 2 * d + 1)]
    values += [los_ref[m] for m in range(3)] + [in_tile.astype(F32)]
    packed = jnp.zeros((64, 128), F32)
    for v, value in enumerate(values):
        high, low = fsplit(value)
        left = jnp.concatenate([row_hot * high, row_hot * low], axis=0).astype(BF16)
        right = hot(iota((128, NY), 0) == place_lane + 4 * v).astype(BF16)
        packed = packed + dot_nt(left, right)
    packed = packed[:32] + packed[32:]
    ms[:, 0] = packed[:16].reshape(16, 1, 128)
    ms[:, 1] = jnp.broadcast_to(block_row.reshape(1, 1, 128), (16, 1, 128))
    ms[:, 2] = packed[16:].reshape(16, 1, 128)
    r1[z] = ms[z]
    for i, peer in enumerate(z_peers):
        started.append(copy(ms.at[z_ids[i]], r1.at[z], 17 + i, peer))
        started[-1].start()

    def weave(plane, index, value, alive):
        if alive is not None:
            value = jnp.where(alive, value, 0.0)
        high, low = split(jnp.concatenate([from_left(value), value], axis=0))
        w[plane, index * 96 : index * 96 + 48] = high
        w[plane, index * 96 + 48 : index * 96 + 96] = low

    for k in range(ROWS):
        weave(1, k + 1, st[k], None)

    order = hot(iota((384, 384), 0) == 3 * (iota((384, 384), 1) % 128) + iota((384, 384), 1) // 128)
    order_t = hot(iota((384, 384), 1) == 3 * (iota((384, 384), 0) % 128) + iota((384, 384), 0) // 128)
    order, order_t = order.astype(BF16), order_t.astype(BF16)
    for i, part in enumerate(split(c_ref[...])):
        c_perm[i] = dot(order_t, dot(part, order).astype(BF16)).astype(BF16)

    for i in range(3):
        copy(own_mod, mod_in.at[i], 3 + i, (down, d)).wait_recv()
    inner = d < ND - 1
    last = s == SLABS - 1
    for k in range(ROWS):
        mods[0, k] = own_mod[k : k + 1, :]
        mods[1, k] = jnp.where(last, 0.0, mod_in[0, k : k + 1, :])
    mods[0, ROWS] = jnp.where(inner, mod_in[1, 0:1, :], 0.0)
    mods[1, ROWS] = jnp.where(inner & jnp.logical_not(last), mod_in[2, 0:1, :], 0.0)

    for i in range(6):
        copy(st.at[0], hz.at[0, 0], 9 + i, (s, higher)).wait_recv()
    not_first, not_last = s > 0, s < SLABS - 1
    weave(1, 0, hz[1, 0], d > 0)
    weave(1, 9, hz[1, 1], inner)

    for i in range(15):
        copy(ms.at[0], r1.at[0], 17 + i, (down, d)).wait_recv()
    for i, peer in enumerate(g_peers):
        half = g_ids[i] // 4
        started.append(copy(r1.at[:, pl.ds(half, 2)], r2.at[x, :, c], 32 + i, peer))
        started[-1].start()
    half = g // 4
    for k in range(NZ):
        r2[x, k, c] = r1[k, pl.ds(half, 2)]

    for k in range(ROWS + 1):
        block = w[1, 96 * k : 96 * k + 192]
        f = dot(lhs_own[0], block) + dot(lhs_own[1], block)
        f_own[k] = mods[0, k] * f[:96] + mods[1, k] * f[96:]

    rho, eps = iota((128, 24), 0), iota((128, 24), 1)
    corner, rest = rho // 32, rho % 32
    comp, plane, comp2 = rest // 9, (rest % 9) // 3, rest % 3
    left = jnp.zeros((128, 8), F32)
    for layer in range(2):
        rows = dot_full(hot((eps == 12 * (1 - layer) + 3 * corner + comp) & (rest < 27)), e)
        keep = (eps % 3 == comp2) & (eps // 12 == plane - layer)
        of, to = iota((24, 8), 0), iota((24, 8), 1)
        gather = hot((to // 4 == layer) & ((of % 12) // 3 == to % 4))
        left = left + dot_full(jnp.where(keep, rows, 0.0), gather)
    high, low = fsplit(left)
    left_high = jnp.concatenate([high, high], axis=1).astype(BF16)
    left_low = jnp.concatenate([low, jnp.zeros_like(low)], axis=1).astype(BF16)
    before = None
    for k in range(ROWS + 1):
        sub, lane = iota((8, NY), 0), iota((8, NY), 1)
        block = jnp.where(sub < 4, mods[0, k], mods[1, k])
        there = (sub % 2 == 1) | (lane > 0)
        if k == 0:
            there = there & ((sub % 4 >= 2) | (d > 0))
        block = jnp.where(there, block, 0.0)
        high, low = fsplit(block)
        block = jnp.concatenate([high, low], axis=0).astype(BF16)
        now = dot(left_high, block) + dot(left_low, block)
        if before is not None:
            both = before[64:] + now[:64]
            g_z[k - 1] = both[32:] + from_right(both[:32])
        before = now

    for i in range(2):
        copy(st, hp.at[i], 15 + i, (down, d)).wait_recv()
    for plane, index, alive in ((0, 0, not_first), (2, 1, not_last)):
        weave(plane, 0, hz[plane, 0], alive & (d > 0))
        weave(plane, 9, hz[plane, 1], alive & inner)
        for k in range(ROWS):
            weave(plane, k + 1, hp[index, k], alive)
    before = None
    for k in range(ROWS + 1):
        now = f_own[k]
        for i in range(2):
            block = w[2 * i, 96 * k : 96 * k + 192]
            now = now + mods[i, k] * (dot(lhs_nb[i, 0], block) + dot(lhs_nb[i, 1], block))
        if before is not None:
            both = before[48:] + now[:48]
            app[k - 1] = both[24:] + from_right(both[:24])
        before = now

    for i in range(7):
        copy(r1.at[:, pl.ds(0, 2)], r2.at[0, :, 0], 32 + i, (down, d)).wait_recv()
    flat = r2.reshape(2 * SLABS, 128)
    means = jnp.transpose(flat[pl.ds(1 - half, SLABS, stride=2), :]) * (1.0 / NODES)
    gps[...] = jnp.transpose(flat[pl.ds(half, SLABS, stride=2), :])
    means = jnp.concatenate([means[m * 8 : m * 8 + 8] for m in range(3)], axis=1)
    high, low = fsplit(means)
    both = jnp.concatenate([high, low], axis=0).astype(BF16)
    solved = dot(both, c_perm[0])
    corr = solved[:8] + solved[8:] + dot(both, c_perm[1])[:8]
    lane = iota((8, 128), 1)
    mine = [
        [
            jnp.sum(
                jnp.where(lane == s + p - 1, corr[:, m * 128 : m * 128 + 128], 0.0),
                axis=1,
                keepdims=True,
            )
            for m in range(3)
        ]
        for p in range(3)
    ]
    own = jnp.concatenate(mine[1], axis=0)
    near_sum = jnp.zeros((24, NY), F32)
    force_sum = jnp.zeros((24, NY), F32)
    for k in range(ROWS):
        grown = []
        for m in range(3):
            total = app[k, m * 8 : m * 8 + 8]
            for p in range(3):
                for m2 in range(3):
                    i = m * 9 + p * 3 + m2
                    total = total + mine[p][m2] * g_z[k, i : i + 1]
            grown.append(total)
        total = jnp.concatenate(grown, axis=0)
        app[k] = total
        direction = st[k] + own
        near_sum = near_sum + direction * total
        force_sum = force_sum + direction * rt[k]
    near_sum = jnp.sum(near_sum, axis=1, keepdims=True)
    force_sum = jnp.sum(force_sum, axis=1, keepdims=True)
    row = to_row(
        [
            force_sum[:8] + force_sum[8:16] + force_sum[16:],
            near_sum[:8] + near_sum[8:16] + near_sum[16:],
        ]
    )

    ly_out[...] = row
    ly_in[d] = row
    for i, peer in enumerate(y_peers):
        started.append(copy(ly_out, ly_in.at[d], 39 + i, peer))
        started[-1].start()

    group = gps[pl.ds(pl.multiple_of((g % 4) * 32, 32), 32), :]
    found = []
    for v in range(2):
        value = group[4 * v : 4 * v + 4]
        for m in range(3):
            value = value + group[8 + 4 * m : 12 + 4 * m] * pick_row(
                corr[:, m * 128 : m * 128 + 128], 2 * d + v
            )
        found.append(jnp.concatenate([value[j : j + 1] for j in range(4)], axis=1))
    ids = group[20:24].astype(jnp.int32)
    sub = iota((8, 512), 0)
    parts = [fsplit(v) for v in found]
    left = jnp.where(sub == 0, parts[0][0], jnp.where(sub == 1, parts[1][0], 0.0))
    left = jnp.where(sub == 2, parts[0][1], jnp.where(sub == 3, parts[1][1], left))
    right = jnp.concatenate([hot(iota((256, 128), 0) == ids[j : j + 1]) for j in range(4)], axis=1)
    bins = dot_nt(left.astype(BF16), right.astype(BF16))

    for i in range(3):
        copy(ly_out, ly_in.at[0], 39 + i, y_peers[i]).wait_recv()
    row = ly_in[0] + ly_in[1] + ly_in[2] + ly_in[3]
    lz_out[...] = row
    lz_in[z] = row
    for i, peer in enumerate(z_peers):
        started.append(copy(lz_out, lz_in.at[z], 42 + i, peer))
        started[-1].start()
    for i in range(15):
        copy(lz_out, lz_in.at[0], 42 + i, (down, d)).wait_recv()
    row = jnp.sum(lz_in[...], axis=0)
    lx_out[...] = row
    lx_in[g] = row
    for i, peer in enumerate(g_peers):
        started.append(copy(lx_out, lx_in.at[g], 57 + i, peer))
        started[-1].start()
    for i in range(7):
        copy(lx_out, lx_in.at[0], 57 + i, (down, d)).wait_recv()
    row = jnp.broadcast_to(jnp.sum(lx_in[...], axis=0), (8, 128))
    lane, sub = iota((8, 128), 1), iota((8, 128), 0)
    numerator = jnp.sum(jnp.where(lane == sub, row, 0.0), axis=1, keepdims=True)
    denominator = jnp.sum(jnp.where(lane == sub + 8, row, 0.0), axis=1, keepdims=True)
    step = numerator / denominator
    steps = jnp.concatenate([step] * 3, axis=0)
    res_ref[...] = jnp.transpose(rt[...] - steps * app[...], (1, 0, 2))
    wide_step = jnp.broadcast_to(step, (8, NY))
    for v in range(2):
        pix_ref[v : v + 1, :] = pick_row(wide_step, 2 * d + v) * (
            bins[v : v + 1] + bins[v + 2 : v + 3]
        )

    for each in started:
        each.wait_send()

    @pl.when(d == ND - 1)
    def _():
        for each in shows():
            each.wait_send()


def body(right_side, smoother, material, moduli, element_matrix, coarse_inverse, surface_map, line_of_sight):
    vmem = pl.BlockSpec(memory_space=pltpu.VMEM)
    smem = pl.BlockSpec(memory_space=pltpu.SMEM)
    residual, pixels = pl.pallas_call(
        kernel,
        out_shape=(
            jax.ShapeDtypeStruct((24, ROWS, NY), F32),
            jax.ShapeDtypeStruct((2, NY), F32),
        ),
        in_specs=[vmem, vmem, vmem, smem, vmem, vmem, vmem, vmem],
        out_specs=(vmem, vmem),
        scratch_shapes=[
            pltpu.VMEM((ROWS, 24, NY), F32),
            pltpu.VMEM((ROWS, 24, NY), F32),
            pltpu.VMEM((2, ROWS, 24, NY), F32),
            pltpu.VMEM((3, 2, 24, NY), F32),
            pltpu.VMEM((ROWS, NY), F32),
            pltpu.VMEM((3, ROWS, NY), F32),
            pltpu.VMEM((2, ROWS + 1, 1, NY), F32),
            pltpu.VMEM((3, 960, NY), BF16),
            pltpu.VMEM((ROWS + 1, 96, NY), F32),
            pltpu.VMEM((2, 192, 192), BF16),
            pltpu.VMEM((2, 2, 96, 192), BF16),
            pltpu.VMEM((ROWS, 24, NY), F32),
            pltpu.VMEM((ROWS, 32, NY), F32),
            pltpu.VMEM((2, 384, 384), BF16),
            pltpu.VMEM((8, NY), F32),
            pltpu.VMEM((8, NY), F32),
            pltpu.VMEM((1, 128), F32),
            pltpu.VMEM((ND, 1, 128), F32),
            pltpu.VMEM((NZ, 3, 1, 128), F32),
            pltpu.VMEM((NZ, 3, 1, 128), F32),
            pltpu.VMEM((NX, NZ, NC, 2, 1, 128), F32),
            pltpu.VMEM((128, 128), F32),
            pltpu.VMEM((1, 128), F32),
            pltpu.VMEM((ND, 1, 128), F32),
            pltpu.VMEM((1, 128), F32),
            pltpu.VMEM((NZ, 1, 128), F32),
            pltpu.VMEM((1, 128), F32),
            pltpu.VMEM((8, 1, 128), F32),
            pltpu.SemaphoreType.DMA((64,)),
            pltpu.SemaphoreType.DMA((64,)),
        ],
        compiler_params=pltpu.CompilerParams(
            collective_id=0, has_side_effects=True, vmem_limit_bytes=40 * 1024 * 1024
        ),
    )(
        right_side.reshape(24, ROWS, NY),
        smoother.reshape(3, ROWS, NY),
        material.reshape(ROWS, NY),
        moduli,
        element_matrix,
        coarse_inverse,
        surface_map,
        line_of_sight,
    )
    return residual.reshape(right_side.shape), pixels


def solution(mesh):
    return jax.shard_map(
        body,
        mesh=mesh,
        in_specs=(
            P(None, None, "slab", "depth", None),
            P(None, "slab", "depth", None),
            P("slab", "depth", None),
            P(),
            P(),
            P(),
            P("slab", None),
            P(None, "slab", None),
        ),
        out_specs=(P(None, None, "slab", "depth", None), P("depth", "slab")),
        check_vma=False,
    )
```

```python
import jax
import jax.numpy as jnp
from jax import lax
from jax.experimental import pallas as pl
from jax.experimental.pallas import tpu as pltpu
from jax.sharding import PartitionSpec as P

F32, BF16 = jnp.float32, jnp.bfloat16
MESH = pl.DeviceIdType.MESH
HIGHEST = lax.Precision.HIGHEST
NX, NZ, NC, ND = 4, 16, 2, 4
SLABS, ROWS, NY = NX * NZ * NC, 8, 256
NODES = ROWS * ND * NY


def iota(shape, dim):
    return lax.broadcasted_iota(jnp.int32, shape, dim)


def dot(a, b):
    return jnp.dot(a, b, preferred_element_type=F32)


def dot_full(a, b):
    return jnp.dot(a, b, preferred_element_type=F32, precision=HIGHEST)


def dot_nt(a, b):
    return lax.dot_general(a, b, (((1,), (1,)), ((), ())), preferred_element_type=F32)


def split(v):
    high = v.astype(BF16)
    return high, (v - high.astype(F32)).astype(BF16)


def fsplit(v):
    high = v.astype(BF16).astype(F32)
    return high, v - high


def hot(mask):
    return jnp.where(mask, 1.0, 0.0).astype(F32)


def from_right(v):
    width = v.shape[1]
    return jnp.where(iota(v.shape, 1) == width - 1, 0.0, pltpu.roll(v, width - 1, axis=1))


def from_left(v):
    return jnp.where(iota(v.shape, 1) == 0, 0.0, pltpu.roll(v, 1, axis=1))


def to_row(columns):
    lane, sub = iota((8, 128), 1), iota((8, 128), 0)
    total = jnp.zeros((8, 128), F32)
    for q, column in enumerate(columns):
        total = jnp.where(lane == q * 8 + sub, column, total)
    return jnp.sum(total, axis=0, keepdims=True)


def pick_row(v, index):
    return jnp.sum(jnp.where(iota(v.shape, 0) == index, v, 0.0), axis=0, keepdims=True)


def kernel(
    r_hbm, s_hbm, mat_hbm, mod_ref, e_hbm, c_hbm, map_hbm, los_hbm,
    res_ref, pix_ref,
    r_ref, s_ref, mat_ref, e_ref, c_ref, map_ref, los_ref,
    rt, st, hp, hz, own_mod, mod_in, mods, w, f_own, lhs_own, lhs_nb, app, g_z,
    c_perm, pj_out, pj_in, px_out, px_mid, px_in, gps,
    y_out, y_in, z_out, z_in, all_in,
    load, send, recv,
):
    s, d = lax.axis_index("slab"), lax.axis_index("depth")
    x, z, c = s // 32, (s // 2) % 16, s % 2
    g = x * 2 + c
    half = g // 4
    up, down = lax.rem(s + 1, SLABS), lax.rem(s + SLABS - 1, SLABS)
    deeper, higher = lax.rem(d + 1, ND), lax.rem(d + ND - 1, ND)

    y_peers = [(s, lax.rem(d + i, ND)) for i in range(1, ND)]
    z_ids = [lax.rem(z + i, NZ) for i in range(1, NZ)]
    z_peers = [(x * 32 + i * 2 + c, d) for i in z_ids]
    g_ids = [lax.rem(g + i, 8) for i in range(1, 8)]
    g_peers = [((i // 2) * 32 + z * 2 + i % 2, d) for i in g_ids]
    near = [(up, d), (down, d)] + [(a, b) for a in (up, down) for b in (deeper, higher)]

    barrier = pltpu.get_barrier_semaphore()
    peers = z_peers + near + y_peers + g_peers
    for peer in peers:
        pl.semaphore_signal(barrier, inc=1, device_id=peer, device_id_type=MESH)

    pairs = [
        (r_hbm, r_ref), (s_hbm, s_ref), (mat_hbm, mat_ref), (los_hbm, los_ref),
        (map_hbm, map_ref), (e_hbm, e_ref), (c_hbm, c_ref),
    ]
    loads = [pltpu.make_async_copy(a, b, load.at[i]) for i, (a, b) in enumerate(pairs)]
    for each in loads:
        each.start()

    def copy(src, dst, index, peer):
        return pltpu.make_async_remote_copy(
            src_ref=src, dst_ref=dst, send_sem=send.at[index], recv_sem=recv.at[index],
            device_id=peer, device_id_type=MESH,
        )

    loads[0].wait()
    loads[1].wait()
    field = jnp.transpose(r_ref[...], (1, 0, 2))
    rt[...] = field
    for k in range(ROWS):
        weight = jnp.concatenate(
            [jnp.broadcast_to(s_ref[m, k : k + 1, :], (8, NY)) for m in range(3)], axis=0
        )
        st[k] = field[k] * weight
    loads[2].wait()
    material = mat_ref[...]
    modulus = jnp.zeros((ROWS, NY), F32)
    for i in range(16):
        modulus = jnp.where(material == i, mod_ref[i], modulus)
    own_mod[...] = modulus
    loads[3].wait()
    shown = jnp.zeros((8, NY), F32)
    for m in range(3):
        shown = shown + los_ref[m] * st[ROWS - 1, m * 8 : m * 8 + 8, :]
    pj_out[...] = shown

    pl.semaphore_wait(barrier, len(peers))

    started = []
    for i, peer in enumerate([(down, d), (s, higher), (down, higher)]):
        started.append(copy(own_mod, mod_in.at[i], 3 + i, peer))
        started[-1].start()
    sides = []
    for plane, a in ((1, s), (2, down), (0, up)):
        sides.append((st.at[0], hz.at[plane, 1], (a, higher)))
        sides.append((st.at[ROWS - 1], hz.at[plane, 0], (a, deeper)))
    for i, (src, dst, peer) in enumerate(sides):
        started.append(copy(src, dst, 9 + i, peer))
        started[-1].start()
    for i, (plane, peer) in enumerate(((1, (down, d)), (0, (up, d)))):
        started.append(copy(st, hp.at[plane], 15 + i, peer))
        started[-1].start()

    def shows():
        return [copy(pj_out, pj_in, 6 + i, (s, i)) for i in range(ND - 1)]

    @pl.when(d == ND - 1)
    def _():
        for each in shows():
            each.start()
        pj_in[...] = shown

    block_sum = jnp.zeros((24, NY), F32)
    force_sum = jnp.zeros((24, NY), F32)
    for k in range(ROWS):
        block_sum = block_sum + rt[k]
        force_sum = force_sum + rt[k] * st[k]
    block_sum = jnp.sum(block_sum, axis=1, keepdims=True)
    force_sum = jnp.sum(force_sum, axis=1, keepdims=True)

    loads[5].wait()
    e = e_ref[...]
    rho, eps = iota((192, 24), 0), iota((192, 24), 1)
    picked = dot_full(hot(eps == (rho % 96) // 8 + 12 * (1 - rho // 96)), e)
    eps, kap = iota((24, 192), 0), iota((24, 192), 1)
    column = 6 * (kap // 96) + (kap % 48) // 8
    wide = [dot_full(picked, hot(eps == column + 12 * a)) for a in range(2)]
    rho, kap = iota((96, 192), 0), iota((96, 192), 1)
    same_source = rho % 8 == kap % 8
    first = same_source & (kap % 96 < 48)
    parts = [wide[1][:96], wide[0][96:], wide[0][:96], wide[1][96:]]
    for i, part in enumerate(parts):
        high, low = fsplit(part)
        high = jnp.where(same_source, high, 0.0).astype(BF16)
        low = jnp.where(first, low, 0.0).astype(BF16)
        if i < 2:
            lhs_own[0, i * 96 : i * 96 + 96] = high
            lhs_own[1, i * 96 : i * 96 + 96] = low
        else:
            lhs_nb[i - 2, 0] = high
            lhs_nb[i - 2, 1] = low

    loads[4].wait()
    target = map_ref[...]
    tile, in_tile = target >> 8, target & 255
    tile_col = jnp.transpose(jnp.broadcast_to(tile.astype(F32), (8, NY)))[:, 0:1]
    same = (tile_col == tile.astype(F32)) & (iota((NY, NY), 0) < iota((NY, NY), 1))
    rank = jnp.sum(hot(same), axis=0, keepdims=True).astype(jnp.int32)
    tile_g = (tile >> 5) * 2 + (tile & 1)
    place_row = (tile_g >> 2) * 16 + ((tile >> 1) & 15)
    place_lane = (tile_g & 3) * 32 + rank
    row_hot = hot(iota((32, NY), 0) == place_row)

    @pl.when(d != ND - 1)
    def _():
        copy(pj_out, pj_in, 6 + d, (s, d)).wait_recv()

    shown = pj_in[...]
    values = [pick_row(shown, 2 * d), pick_row(shown, 2 * d + 1)]
    values += [los_ref[m] for m in range(3)] + [in_tile.astype(F32)]
    packed = jnp.zeros((64, 128), F32)
    for v, value in enumerate(values):
        high, low = fsplit(value)
        left = jnp.concatenate([row_hot * high, row_hot * low], axis=0).astype(BF16)
        right = hot(iota((128, NY), 0) == place_lane + 4 * v).astype(BF16)
        packed = packed + dot_nt(left, right)
    packed = packed[:32] + packed[32:]
    px_out[:, 0] = packed[:16].reshape(16, 1, 128)
    px_out[:, 1] = packed[16:].reshape(16, 1, 128)
    px_mid[z] = px_out[z]
    for i, peer in enumerate(z_peers):
        started.append(copy(px_out.at[z_ids[i]], px_mid.at[z], 17 + i, peer))
        started[-1].start()

    def weave(plane, index, value, alive):
        if alive is not None:
            value = jnp.where(alive, value, 0.0)
        high, low = split(jnp.concatenate([from_left(value), value], axis=0))
        w[plane, index * 96 : index * 96 + 48] = high
        w[plane, index * 96 + 48 : index * 96 + 96] = low

    for k in range(ROWS):
        weave(1, k + 1, st[k], None)

    for i in range(3):
        copy(own_mod, mod_in.at[i], 3 + i, (down, d)).wait_recv()
    inner = d < ND - 1
    last = s == SLABS - 1
    for k in range(ROWS):
        mods[0, k] = own_mod[k : k + 1, :]
        mods[1, k] = jnp.where(last, 0.0, mod_in[0, k : k + 1, :])
    mods[0, ROWS] = jnp.where(inner, mod_in[1, 0:1, :], 0.0)
    mods[1, ROWS] = jnp.where(inner & jnp.logical_not(last), mod_in[2, 0:1, :], 0.0)

    rho, eps = iota((128, 24), 0), iota((128, 24), 1)
    corner, rest = rho // 32, rho % 32
    comp, plane, comp2 = rest // 9, (rest % 9) // 3, rest % 3
    left = jnp.zeros((128, 8), F32)
    for layer in range(2):
        rows = dot_full(hot((eps == 12 * (1 - layer) + 3 * corner + comp) & (rest < 27)), e)
        keep = (eps % 3 == comp2) & (eps // 12 == plane - layer)
        of, to = iota((24, 8), 0), iota((24, 8), 1)
        gather = hot((to // 4 == layer) & ((of % 12) // 3 == to % 4))
        left = left + dot_full(jnp.where(keep, rows, 0.0), gather)
    high, low = fsplit(left)
    left_high = jnp.concatenate([high, high], axis=1).astype(BF16)
    left_low = jnp.concatenate([low, jnp.zeros_like(low)], axis=1).astype(BF16)
    before = None
    unit_sum = jnp.zeros((32, NY), F32)
    for k in range(ROWS + 1):
        sub, lane = iota((8, NY), 0), iota((8, NY), 1)
        block = jnp.where(sub < 4, mods[0, k], mods[1, k])
        there = (sub % 2 == 1) | (lane > 0)
        if k == 0:
            there = there & ((sub % 4 >= 2) | (d > 0))
        block = jnp.where(there, block, 0.0)
        high, low = fsplit(block)
        block = jnp.concatenate([high, low], axis=0).astype(BF16)
        now = dot(left_high, block) + dot(left_low, block)
        if before is not None:
            both = before[64:] + now[:64]
            both = both[32:] + from_right(both[:32])
            g_z[k - 1] = both
            unit_sum = unit_sum + both
        before = now
    unit_sum = jnp.sum(unit_sum, axis=1, keepdims=True)

    for i in range(6):
        copy(st.at[0], hz.at[0, 0], 9 + i, (s, higher)).wait_recv()
    not_first, not_last = s > 0, s < SLABS - 1
    weave(1, 0, hz[1, 0], d > 0)
    weave(1, 9, hz[1, 1], inner)
    for k in range(ROWS + 1):
        block = w[1, 96 * k : 96 * k + 192]
        f = dot(lhs_own[0], block) + dot(lhs_own[1], block)
        f_own[k] = mods[0, k] * f[:96] + mods[1, k] * f[96:]

    for i in range(2):
        copy(st, hp.at[i], 15 + i, (down, d)).wait_recv()
    for plane, index, alive in ((0, 0, not_first), (2, 1, not_last)):
        weave(plane, 0, hz[plane, 0], alive & (d > 0))
        weave(plane, 9, hz[plane, 1], alive & inner)
        for k in range(ROWS):
            weave(plane, k + 1, hp[index, k], alive)
    before = None
    near_sum = jnp.zeros((24, NY), F32)
    cross_sum = jnp.zeros((24, NY), F32)
    for k in range(ROWS + 1):
        now = f_own[k]
        for i in range(2):
            block = w[2 * i, 96 * k : 96 * k + 192]
            now = now + mods[i, k] * (dot(lhs_nb[i, 0], block) + dot(lhs_nb[i, 1], block))
        if before is not None:
            both = before[48:] + now[:48]
            both = both[24:] + from_right(both[:24])
            app[k - 1] = both
            near_sum = near_sum + both * st[k - 1]
            cross_sum = cross_sum + both
        before = now
    near_sum = jnp.sum(near_sum, axis=1, keepdims=True)
    cross_sum = jnp.sum(cross_sum, axis=1, keepdims=True)

    def thirds(v):
        return [v[m * 8 : m * 8 + 8] for m in range(3)]

    row = to_row(
        thirds(block_sum)
        + [sum(thirds(force_sum)), sum(thirds(near_sum))]
        + thirds(cross_sum)
        + [unit_sum[i * 8 : i * 8 + 8] for i in range(4)]
    )
    y_out[...] = row
    y_in[d] = row
    for i, peer in enumerate(y_peers):
        started.append(copy(y_out, y_in.at[d], i, peer))
        started[-1].start()

    for i in range(15):
        copy(px_out.at[0], px_mid.at[0], 17 + i, (down, d)).wait_recv()
    for i, peer in enumerate(g_peers):
        started.append(copy(px_mid.at[:, g_ids[i] // 4], px_in.at[x, :, c], 32 + i, peer))
        started[-1].start()
    for k in range(NZ):
        px_in[x, k, c] = px_mid[k, half]

    for i in range(3):
        copy(y_out, y_in.at[0], i, y_peers[i]).wait_recv()
    row = y_in[0] + y_in[1] + y_in[2] + y_in[3]
    z_out[...] = row
    z_in[z] = row
    for i, peer in enumerate(z_peers):
        started.append(copy(z_out, z_in.at[z], 39 + i, peer))
        started[-1].start()

    loads[6].wait()
    order = hot(iota((384, 384), 0) == 3 * (iota((384, 384), 1) % 128) + iota((384, 384), 1) // 128)
    order_t = hot(iota((384, 384), 1) == 3 * (iota((384, 384), 0) % 128) + iota((384, 384), 0) // 128)
    order, order_t = order.astype(BF16), order_t.astype(BF16)
    for i, part in enumerate(split(c_ref[...])):
        c_perm[i] = dot(order_t, dot(part, order).astype(BF16)).astype(BF16)

    for i in range(7):
        copy(px_mid.at[:, 0], px_in.at[0, :, 0], 32 + i, (down, d)).wait_recv()
    gps[...] = jnp.transpose(px_in.reshape(SLABS, 128)[...])
    group = gps[pl.ds(pl.multiple_of((g % 4) * 32, 32), 32), :]
    ids = group[20:24].astype(jnp.int32)
    bins_right = jnp.concatenate(
        [hot(iota((256, 128), 0) == ids[j : j + 1]) for j in range(4)], axis=1
    ).astype(BF16)

    for i in range(15):
        copy(z_out, z_in.at[0], 39 + i, (down, d)).wait_recv()
    for i, peer in enumerate(g_peers):
        started.append(copy(z_in, all_in.at[x, :, c], 54 + i, peer))
        started[-1].start()
    for k in range(NZ):
        all_in[x, k, c] = z_in[k]
    for i in range(7):
        copy(z_in, all_in.at[0, :, 0], 54 + i, (down, d)).wait_recv()

    slabs = jnp.transpose(all_in.reshape(SLABS, 128)[...])
    sums = [slabs[q * 8 : q * 8 + 8] for q in range(8)]
    means = jnp.concatenate(sums[:3], axis=1) * (1.0 / NODES)
    high, low = fsplit(means)
    both = jnp.concatenate([high, low], axis=0).astype(BF16)
    solved = dot(both, c_perm[0])
    corr = solved[:8] + solved[8:] + dot(both, c_perm[1])[:8]
    corr = [corr[:, m * 128 : m * 128 + 128] for m in range(3)]

    shifted = [[from_left(v) for v in corr], corr, [from_right(v) for v in corr]]
    numerator, denominator = sums[3], sums[4]
    for m in range(3):
        numerator = numerator + corr[m] * sums[m]
        part = 2.0 * sums[5 + m]
        for p in range(3):
            for m2 in range(3):
                i = 64 + m * 9 + p * 3 + m2
                part = part + slabs[i : i + 1] * shifted[p][m2]
        denominator = denominator + corr[m] * part
    step = jnp.sum(numerator, axis=1, keepdims=True) / jnp.sum(denominator, axis=1, keepdims=True)
    lane = iota((8, 128), 1)
    mine = [
        [jnp.sum(jnp.where(lane == s, v, 0.0), axis=1, keepdims=True) for v in shifted[p]]
        for p in range(3)
    ]
    steps = jnp.concatenate([step] * 3, axis=0)
    for k in range(ROWS):
        grown = []
        for m in range(3):
            total = app[k, m * 8 : m * 8 + 8]
            for p in range(3):
                for m2 in range(3):
                    i = m * 9 + p * 3 + m2
                    total = total + mine[p][m2] * g_z[k, i : i + 1]
            grown.append(total)
        app[k] = rt[k] - steps * jnp.concatenate(grown, axis=0)
    res_ref[...] = jnp.transpose(app[...], (1, 0, 2))

    found = []
    for v in range(2):
        value = group[4 * v : 4 * v + 4]
        for m in range(3):
            value = value + group[8 + 4 * m : 12 + 4 * m] * pick_row(corr[m], 2 * d + v)
        found.append(jnp.concatenate([value[j : j + 1] for j in range(4)], axis=1))
    sub = iota((8, 512), 0)
    parts = [fsplit(v) for v in found]
    left = jnp.where(sub == 0, parts[0][0], jnp.where(sub == 1, parts[1][0], 0.0))
    left = jnp.where(sub == 2, parts[0][1], jnp.where(sub == 3, parts[1][1], left))
    bins = dot_nt(left.astype(BF16), bins_right)
    wide_step = jnp.broadcast_to(step, (8, NY))
    for v in range(2):
        pix_ref[v : v + 1, :] = pick_row(wide_step, 2 * d + v) * (
            bins[v : v + 1] + bins[v + 2 : v + 3]
        )

    for each in started:
        each.wait_send()

    @pl.when(d == ND - 1)
    def _():
        for each in shows():
            each.wait_send()


def body(right_side, smoother, material, moduli, element_matrix, coarse_inverse, surface_map, line_of_sight):
    vmem = pl.BlockSpec(memory_space=pltpu.VMEM)
    smem = pl.BlockSpec(memory_space=pltpu.SMEM)
    hbm = pl.BlockSpec(memory_space=pltpu.HBM)
    residual, pixels = pl.pallas_call(
        kernel,
        out_shape=(
            jax.ShapeDtypeStruct((24, ROWS, NY), F32),
            jax.ShapeDtypeStruct((2, NY), F32),
        ),
        in_specs=[hbm, hbm, hbm, smem, hbm, hbm, hbm, hbm],
        out_specs=(vmem, vmem),
        scratch_shapes=[
            pltpu.VMEM((24, ROWS, NY), F32),
            pltpu.VMEM((3, ROWS, NY), F32),
            pltpu.VMEM((ROWS, NY), jnp.int32),
            pltpu.VMEM((24, 24), F32),
            pltpu.VMEM((384, 384), F32),
            pltpu.VMEM((1, NY), jnp.int32),
            pltpu.VMEM((3, 1, NY), F32),
            pltpu.VMEM((ROWS, 24, NY), F32),
            pltpu.VMEM((ROWS, 24, NY), F32),
            pltpu.VMEM((2, ROWS, 24, NY), F32),
            pltpu.VMEM((3, 2, 24, NY), F32),
            pltpu.VMEM((ROWS, NY), F32),
            pltpu.VMEM((3, ROWS, NY), F32),
            pltpu.VMEM((2, ROWS + 1, 1, NY), F32),
            pltpu.VMEM((3, 960, NY), BF16),
            pltpu.VMEM((ROWS + 1, 96, NY), F32),
            pltpu.VMEM((2, 192, 192), BF16),
            pltpu.VMEM((2, 2, 96, 192), BF16),
            pltpu.VMEM((ROWS, 24, NY), F32),
            pltpu.VMEM((ROWS, 32, NY), F32),
            pltpu.VMEM((2, 384, 384), BF16),
            pltpu.VMEM((8, NY), F32),
            pltpu.VMEM((8, NY), F32),
            pltpu.VMEM((NZ, 2, 1, 128), F32),
            pltpu.VMEM((NZ, 2, 1, 128), F32),
            pltpu.VMEM((NX, NZ, NC, 1, 128), F32),
            pltpu.VMEM((128, 128), F32),
            pltpu.VMEM((1, 128), F32),
            pltpu.VMEM((ND, 1, 128), F32),
            pltpu.VMEM((1, 128), F32),
            pltpu.VMEM((NZ, 1, 128), F32),
            pltpu.VMEM((NX, NZ, NC, 1, 128), F32),
            pltpu.SemaphoreType.DMA((7,)),
            pltpu.SemaphoreType.DMA((61,)),
            pltpu.SemaphoreType.DMA((61,)),
        ],
        compiler_params=pltpu.CompilerParams(
            collective_id=0, has_side_effects=True, vmem_limit_bytes=60 * 1024 * 1024
        ),
    )(
        right_side.reshape(24, ROWS, NY),
        smoother.reshape(3, ROWS, NY),
        material.reshape(ROWS, NY),
        moduli,
        element_matrix,
        coarse_inverse,
        surface_map,
        line_of_sight,
    )
    return residual.reshape(right_side.shape), pixels


def solution(mesh):
    return jax.shard_map(
        body,
        mesh=mesh,
        in_specs=(
            P(None, None, "slab", "depth", None),
            P(None, "slab", "depth", None),
            P("slab", "depth", None),
            P(),
            P(),
            P(),
            P("slab", None),
            P(None, "slab", None),
        ),
        out_specs=(P(None, None, "slab", "depth", None), P("depth", "slab")),
        check_vma=False,
    )
```

```python
import jax
import jax.numpy as jnp
from jax import lax
from jax.experimental import pallas as pl
from jax.experimental.pallas import tpu as pltpu
from jax.sharding import PartitionSpec as P

F32, BF16 = jnp.float32, jnp.bfloat16
MESH = pl.DeviceIdType.MESH
HIGHEST = lax.Precision.HIGHEST
NX, NZ, NC, ND = 4, 16, 2, 4
SLABS, ROWS, NY = NX * NZ * NC, 8, 256
NODES = ROWS * ND * NY


def iota(shape, dim):
    return lax.broadcasted_iota(jnp.int32, shape, dim)


def dot(a, b):
    return jnp.dot(a, b, preferred_element_type=F32)


def dot_full(a, b):
    return jnp.dot(a, b, preferred_element_type=F32, precision=HIGHEST)


def dot_nt(a, b):
    return lax.dot_general(a, b, (((1,), (1,)), ((), ())), preferred_element_type=F32)


def split(v):
    high = v.astype(BF16)
    return high, (v - high.astype(F32)).astype(BF16)


def fsplit(v):
    high = v.astype(BF16).astype(F32)
    return high, v - high


def hot(mask):
    return jnp.where(mask, 1.0, 0.0).astype(F32)


def from_right(v):
    width = v.shape[1]
    return jnp.where(iota(v.shape, 1) == width - 1, 0.0, pltpu.roll(v, width - 1, axis=1))


def from_left(v):
    return jnp.where(iota(v.shape, 1) == 0, 0.0, pltpu.roll(v, 1, axis=1))


def to_row(columns):
    lane, sub = iota((8, 128), 1), iota((8, 128), 0)
    total = jnp.zeros((8, 128), F32)
    for q, column in enumerate(columns):
        total = jnp.where(lane == q * 8 + sub, column, total)
    return jnp.sum(total, axis=0, keepdims=True)


def pick_row(v, index):
    return jnp.sum(jnp.where(iota(v.shape, 0) == index, v, 0.0), axis=0, keepdims=True)


def kernel(
    r_hbm, s_hbm, mat_hbm, mod_ref, e_hbm, c_hbm, map_hbm, los_hbm,
    res_ref, pix_ref,
    r_ref, s_ref, mat_ref, e_ref, c_ref, map_ref, los_ref,
    rt, st, hp, hz, own_mod, mod_in, mods, w, f_own, lhs_own, lhs_nb, app, g_z,
    c_perm, pj_out, pj_in, px_out, px_raw, px_relay, px_mid, px_in, ordered, gps,
    y_out, y_in, z_out, all_in,
    load, send, recv,
):
    s, d = lax.axis_index("slab"), lax.axis_index("depth")
    x, z, c = s // 32, (s // 2) % 16, s % 2
    g = x * 2 + c
    half = g // 4
    up, down = lax.rem(s + 1, SLABS), lax.rem(s + SLABS - 1, SLABS)
    deeper, higher = lax.rem(d + 1, ND), lax.rem(d + ND - 1, ND)

    z_id = {j: lax.rem(z + j + NZ, NZ) for j in range(-8, 9)}
    z_steps = [1, 2, 3, 4, -1, -2, -3, -4]
    z_peer = {j: (x * 32 + z_id[j] * 2 + c, d) for j in z_steps}
    g_ids = [lax.rem(g + i, 8) for i in range(1, 8)]
    g_peers = [((i // 2) * 32 + z * 2 + i % 2, d) for i in g_ids]
    layer_peers = []
    for i in range(1, 32):
        h = lax.rem(g + i // ND, 8)
        layer_peers.append(((h // 2) * 32 + z * 2 + h % 2, lax.rem(d + i % ND, ND)))
    near = [(up, d), (down, d)] + [(a, b) for a in (up, down) for b in (deeper, higher)]

    barrier = pltpu.get_barrier_semaphore()
    peers = list(z_peer.values()) + near + layer_peers
    for peer in peers:
        pl.semaphore_signal(barrier, inc=1, device_id=peer, device_id_type=MESH)

    pairs = [
        (r_hbm, r_ref), (s_hbm, s_ref), (mat_hbm, mat_ref), (los_hbm, los_ref),
        (map_hbm, map_ref), (e_hbm, e_ref), (c_hbm, c_ref),
    ]
    loads = [pltpu.make_async_copy(a, b, load.at[i]) for i, (a, b) in enumerate(pairs)]
    for each in loads:
        each.start()

    def copy(src, dst, index, peer):
        return pltpu.make_async_remote_copy(
            src_ref=src, dst_ref=dst, send_sem=send.at[index], recv_sem=recv.at[index],
            device_id=peer, device_id_type=MESH,
        )

    loads[0].wait()
    loads[1].wait()
    field = jnp.transpose(r_ref[...], (1, 0, 2))
    rt[...] = field
    for k in range(ROWS):
        weight = jnp.concatenate(
            [jnp.broadcast_to(s_ref[m, k : k + 1, :], (8, NY)) for m in range(3)], axis=0
        )
        st[k] = field[k] * weight
    loads[2].wait()
    material = mat_ref[...]
    modulus = jnp.zeros((ROWS, NY), F32)
    for i in range(16):
        modulus = jnp.where(material == i, mod_ref[i], modulus)
    own_mod[...] = modulus
    loads[3].wait()
    shown = jnp.zeros((8, NY), F32)
    for m in range(3):
        shown = shown + los_ref[m] * st[ROWS - 1, m * 8 : m * 8 + 8, :]
    pj_out[...] = shown

    pl.semaphore_wait(barrier, len(peers))

    started = []
    for i, peer in enumerate([(down, d), (s, higher), (down, higher)]):
        started.append(copy(own_mod, mod_in.at[i], 3 + i, peer))
        started[-1].start()
    sides = []
    for plane, a in ((1, s), (2, down), (0, up)):
        sides.append((st.at[0], hz.at[plane, 1], (a, higher)))
        sides.append((st.at[ROWS - 1], hz.at[plane, 0], (a, deeper)))
    for i, (src, dst, peer) in enumerate(sides):
        started.append(copy(src, dst, 9 + i, peer))
        started[-1].start()
    for i, (plane, peer) in enumerate(((1, (down, d)), (0, (up, d)))):
        started.append(copy(st, hp.at[plane], 15 + i, peer))
        started[-1].start()

    def shows():
        return [copy(pj_out, pj_in, 6 + i, (s, i)) for i in range(ND - 1)]

    @pl.when(d == ND - 1)
    def _():
        for each in shows():
            each.start()
        pj_in[...] = shown

    block_sum = jnp.zeros((24, NY), F32)
    force_sum = jnp.zeros((24, NY), F32)
    for k in range(ROWS):
        block_sum = block_sum + rt[k]
        force_sum = force_sum + rt[k] * st[k]
    block_sum = jnp.sum(block_sum, axis=1, keepdims=True)
    force_sum = jnp.sum(force_sum, axis=1, keepdims=True)

    loads[5].wait()
    e = e_ref[...]
    rho, eps = iota((192, 24), 0), iota((192, 24), 1)
    picked = dot_full(hot(eps == (rho % 96) // 8 + 12 * (1 - rho // 96)), e)
    eps, kap = iota((24, 192), 0), iota((24, 192), 1)
    column = 6 * (kap // 96) + (kap % 48) // 8
    wide = [dot_full(picked, hot(eps == column + 12 * a)) for a in range(2)]
    rho, kap = iota((96, 192), 0), iota((96, 192), 1)
    same_source = rho % 8 == kap % 8
    first = same_source & (kap % 96 < 48)
    parts = [wide[1][:96], wide[0][96:], wide[0][:96], wide[1][96:]]
    for i, part in enumerate(parts):
        high, low = fsplit(part)
        high = jnp.where(same_source, high, 0.0).astype(BF16)
        low = jnp.where(first, low, 0.0).astype(BF16)
        if i < 2:
            lhs_own[0, i * 96 : i * 96 + 96] = high
            lhs_own[1, i * 96 : i * 96 + 96] = low
        else:
            lhs_nb[i - 2, 0] = high
            lhs_nb[i - 2, 1] = low

    loads[4].wait()
    target = map_ref[...]
    tile, in_tile = target >> 8, target & 255
    tile_col = jnp.transpose(jnp.broadcast_to(tile.astype(F32), (8, NY)))[:, 0:1]
    same = (tile_col == tile.astype(F32)) & (iota((NY, NY), 0) < iota((NY, NY), 1))
    rank = jnp.sum(hot(same), axis=0, keepdims=True).astype(jnp.int32)
    tile_g = (tile >> 5) * 2 + (tile & 1)
    place_row = (tile_g >> 2) * 16 + ((tile >> 1) & 15)
    place_lane = (tile_g & 3) * 32 + rank
    row_hot = hot(iota((32, NY), 0) == place_row)

    far = [5, 6, 7, 8, -5, -6, -7]

    @pl.when(d != ND - 1)
    def _():
        copy(pj_out, pj_in, 6 + d, (s, d)).wait_recv()

    shown = pj_in[...]
    values = [pick_row(shown, 2 * d), pick_row(shown, 2 * d + 1)]
    values += [los_ref[m] for m in range(3)] + [in_tile.astype(F32)]
    packed = jnp.zeros((64, 128), F32)
    for v, value in enumerate(values):
        high, low = fsplit(value)
        left = jnp.concatenate([row_hot * high, row_hot * low], axis=0).astype(BF16)
        right = hot(iota((128, NY), 0) == place_lane + 4 * v).astype(BF16)
        packed = packed + dot_nt(left, right)
    packed = packed[:32] + packed[32:]
    px_out[:, 0] = packed[:16].reshape(16, 1, 128)
    px_out[:, 1] = packed[16:].reshape(16, 1, 128)
    px_raw[z] = px_out[z]
    for i, j in enumerate(z_steps):
        started.append(copy(px_out.at[z_id[j]], px_raw.at[z], 17 + i, z_peer[j]))
        started[-1].start()
    for i, j in enumerate(far):
        peer = z_peer[4 if j > 0 else -4]
        started.append(copy(px_out.at[z_id[j]], px_relay.at[i], 25 + i, peer))
        started[-1].start()

    def weave(plane, index, value, alive):
        if alive is not None:
            value = jnp.where(alive, value, 0.0)
        high, low = split(jnp.concatenate([from_left(value), value], axis=0))
        w[plane, index * 96 : index * 96 + 48] = high
        w[plane, index * 96 + 48 : index * 96 + 96] = low

    for k in range(ROWS):
        weave(1, k + 1, st[k], None)

    for i in range(3):
        copy(own_mod, mod_in.at[i], 3 + i, (down, d)).wait_recv()
    inner = d < ND - 1
    last = s == SLABS - 1
    for k in range(ROWS):
        mods[0, k] = own_mod[k : k + 1, :]
        mods[1, k] = jnp.where(last, 0.0, mod_in[0, k : k + 1, :])
    mods[0, ROWS] = jnp.where(inner, mod_in[1, 0:1, :], 0.0)
    mods[1, ROWS] = jnp.where(inner & jnp.logical_not(last), mod_in[2, 0:1, :], 0.0)

    rho, eps = iota((128, 24), 0), iota((128, 24), 1)
    corner, rest = rho // 32, rho % 32
    comp, plane, comp2 = rest // 9, (rest % 9) // 3, rest % 3
    left = jnp.zeros((128, 8), F32)
    for layer in range(2):
        rows = dot_full(hot((eps == 12 * (1 - layer) + 3 * corner + comp) & (rest < 27)), e)
        keep = (eps % 3 == comp2) & (eps // 12 == plane - layer)
        of, to = iota((24, 8), 0), iota((24, 8), 1)
        gather = hot((to // 4 == layer) & ((of % 12) // 3 == to % 4))
        left = left + dot_full(jnp.where(keep, rows, 0.0), gather)
    high, low = fsplit(left)
    left_high = jnp.concatenate([high, high], axis=1).astype(BF16)
    left_low = jnp.concatenate([low, jnp.zeros_like(low)], axis=1).astype(BF16)
    before = None
    unit_sum = jnp.zeros((32, NY), F32)
    for k in range(ROWS + 1):
        sub, lane = iota((8, NY), 0), iota((8, NY), 1)
        block = jnp.where(sub < 4, mods[0, k], mods[1, k])
        there = (sub % 2 == 1) | (lane > 0)
        if k == 0:
            there = there & ((sub % 4 >= 2) | (d > 0))
        block = jnp.where(there, block, 0.0)
        high, low = fsplit(block)
        block = jnp.concatenate([high, low], axis=0).astype(BF16)
        now = dot(left_high, block) + dot(left_low, block)
        if before is not None:
            both = before[64:] + now[:64]
            both = both[32:] + from_right(both[:32])
            g_z[k - 1] = both
            unit_sum = unit_sum + both
        before = now
    unit_sum = jnp.sum(unit_sum, axis=1, keepdims=True)

    for i in range(6):
        copy(st.at[0], hz.at[0, 0], 9 + i, (s, higher)).wait_recv()
    not_first, not_last = s > 0, s < SLABS - 1
    weave(1, 0, hz[1, 0], d > 0)
    weave(1, 9, hz[1, 1], inner)
    for k in range(ROWS + 1):
        block = w[1, 96 * k : 96 * k + 192]
        f = dot(lhs_own[0], block) + dot(lhs_own[1], block)
        f_own[k] = mods[0, k] * f[:96] + mods[1, k] * f[96:]

    for i in range(7):
        copy(px_out.at[0], px_relay.at[0], 25 + i, (down, d)).wait_recv()
    for i, j in enumerate(far):
        origin, peer = (z_id[-4], z_peer[j - 4]) if j > 0 else (z_id[4], z_peer[j + 4])
        started.append(copy(px_relay.at[i], px_raw.at[origin], 39 + i, peer))
        started[-1].start()

    for i in range(2):
        copy(st, hp.at[i], 15 + i, (down, d)).wait_recv()
    for plane, index, alive in ((0, 0, not_first), (2, 1, not_last)):
        weave(plane, 0, hz[plane, 0], alive & (d > 0))
        weave(plane, 9, hz[plane, 1], alive & inner)
        for k in range(ROWS):
            weave(plane, k + 1, hp[index, k], alive)
    before = None
    near_sum = jnp.zeros((24, NY), F32)
    cross_sum = jnp.zeros((24, NY), F32)
    for k in range(ROWS + 1):
        now = f_own[k]
        for i in range(2):
            block = w[2 * i, 96 * k : 96 * k + 192]
            now = now + mods[i, k] * (dot(lhs_nb[i, 0], block) + dot(lhs_nb[i, 1], block))
        if before is not None:
            both = before[48:] + now[:48]
            both = both[24:] + from_right(both[:24])
            app[k - 1] = both
            near_sum = near_sum + both * st[k - 1]
            cross_sum = cross_sum + both
        before = now
    near_sum = jnp.sum(near_sum, axis=1, keepdims=True)
    cross_sum = jnp.sum(cross_sum, axis=1, keepdims=True)

    def thirds(v):
        return [v[m * 8 : m * 8 + 8] for m in range(3)]

    row = to_row(
        thirds(block_sum)
        + [sum(thirds(force_sum)), sum(thirds(near_sum))]
        + thirds(cross_sum)
        + [unit_sum[i * 8 : i * 8 + 8] for i in range(4)]
    )
    y_out[...] = row
    y_in[g, d] = row
    for i, peer in enumerate(layer_peers):
        started.append(copy(y_out, y_in.at[g, d], 61 + i, peer))
        started[-1].start()

    for i in range(8):
        copy(px_out.at[0], px_raw.at[0], 17 + i, (down, d)).wait_recv()
    for i in range(7):
        copy(px_relay.at[0], px_raw.at[0], 39 + i, (down, d)).wait_recv()
    pairs = px_raw.reshape(2 * NZ, 128)
    for i in range(2):
        px_mid[i] = pairs[pl.ds(i, NZ, stride=2), :]
    for i, peer in enumerate(g_peers):
        started.append(copy(px_mid.at[g_ids[i] // 4], px_in.at[g], 32 + i, peer))
        started[-1].start()
    px_in[g] = px_mid[half]

    for i in range(31):
        copy(y_out, y_in.at[0, 0], 61 + i, (down, d)).wait_recv()
    rows = y_in[:, 0] + y_in[:, 1] + y_in[:, 2] + y_in[:, 3]
    z_out[...] = rows
    all_in[z] = rows
    for i, j in enumerate(z_steps):
        started.append(copy(z_out, all_in.at[z], 46 + i, z_peer[j]))
        started[-1].start()

    loads[6].wait()
    order = hot(iota((384, 384), 0) == 3 * (iota((384, 384), 1) % 128) + iota((384, 384), 1) // 128)
    order_t = hot(iota((384, 384), 1) == 3 * (iota((384, 384), 0) % 128) + iota((384, 384), 0) // 128)
    order, order_t = order.astype(BF16), order_t.astype(BF16)
    for i, part in enumerate(split(c_ref[...])):
        c_perm[i] = dot(order_t, dot(part, order).astype(BF16)).astype(BF16)

    for i in range(7):
        copy(px_mid.at[0], px_in.at[0], 32 + i, (down, d)).wait_recv()
    for i in range(8):
        ordered[0, pl.ds((i // 2) * 32 + i % 2, NZ, stride=2), :] = px_in[i]
    gps[...] = jnp.transpose(ordered[0])
    group = gps[pl.ds(pl.multiple_of((g % 4) * 32, 32), 32), :]
    ids = group[20:24].astype(jnp.int32)
    bins_right = jnp.concatenate(
        [hot(iota((256, 128), 0) == ids[j : j + 1]) for j in range(4)], axis=1
    ).astype(BF16)

    for i in range(8):
        copy(z_out, all_in.at[0], 46 + i, (down, d)).wait_recv()
    for i, j in enumerate([1, 2, 3, 4, -1, -2, -3]):
        block = all_in.at[z_id[j]]
        started.append(copy(block, block, 54 + i, z_peer[-4 if j > 0 else 4]))
        started[-1].start()
    for i in range(7):
        copy(z_out, all_in.at[0], 54 + i, (down, d)).wait_recv()

    gathered = all_in.reshape(SLABS, 128)
    for i in range(8):
        ordered[1, pl.ds((i // 2) * 32 + i % 2, NZ, stride=2), :] = gathered[pl.ds(i, NZ, stride=8), :]
    slabs = jnp.transpose(ordered[1])
    sums = [slabs[q * 8 : q * 8 + 8] for q in range(8)]
    means = jnp.concatenate(sums[:3], axis=1) * (1.0 / NODES)
    high, low = fsplit(means)
    both = jnp.concatenate([high, low], axis=0).astype(BF16)
    solved = dot(both, c_perm[0])
    corr = solved[:8] + solved[8:] + dot(both, c_perm[1])[:8]
    corr = [corr[:, m * 128 : m * 128 + 128] for m in range(3)]

    shifted = [[from_left(v) for v in corr], corr, [from_right(v) for v in corr]]
    numerator, denominator = sums[3], sums[4]
    for m in range(3):
        numerator = numerator + corr[m] * sums[m]
        part = 2.0 * sums[5 + m]
        for p in range(3):
            for m2 in range(3):
                i = 64 + m * 9 + p * 3 + m2
                part = part + slabs[i : i + 1] * shifted[p][m2]
        denominator = denominator + corr[m] * part
    step = jnp.sum(numerator, axis=1, keepdims=True) / jnp.sum(denominator, axis=1, keepdims=True)
    lane = iota((8, 128), 1)
    mine = [
        [jnp.sum(jnp.where(lane == s, v, 0.0), axis=1, keepdims=True) for v in shifted[p]]
        for p in range(3)
    ]
    steps = jnp.concatenate([step] * 3, axis=0)
    for k in range(ROWS):
        grown = []
        for m in range(3):
            total = app[k, m * 8 : m * 8 + 8]
            for p in range(3):
                for m2 in range(3):
                    i = m * 9 + p * 3 + m2
                    total = total + mine[p][m2] * g_z[k, i : i + 1]
            grown.append(total)
        app[k] = rt[k] - steps * jnp.concatenate(grown, axis=0)
    res_ref[...] = jnp.transpose(app[...], (1, 0, 2))

    found = []
    for v in range(2):
        value = group[4 * v : 4 * v + 4]
        for m in range(3):
            value = value + group[8 + 4 * m : 12 + 4 * m] * pick_row(corr[m], 2 * d + v)
        found.append(jnp.concatenate([value[j : j + 1] for j in range(4)], axis=1))
    sub = iota((8, 512), 0)
    parts = [fsplit(v) for v in found]
    left = jnp.where(sub == 0, parts[0][0], jnp.where(sub == 1, parts[1][0], 0.0))
    left = jnp.where(sub == 2, parts[0][1], jnp.where(sub == 3, parts[1][1], left))
    bins = dot_nt(left.astype(BF16), bins_right)
    wide_step = jnp.broadcast_to(step, (8, NY))
    for v in range(2):
        pix_ref[v : v + 1, :] = pick_row(wide_step, 2 * d + v) * (
            bins[v : v + 1] + bins[v + 2 : v + 3]
        )

    for each in started:
        each.wait_send()

    @pl.when(d == ND - 1)
    def _():
        for each in shows():
            each.wait_send()


def body(right_side, smoother, material, moduli, element_matrix, coarse_inverse, surface_map, line_of_sight):
    vmem = pl.BlockSpec(memory_space=pltpu.VMEM)
    smem = pl.BlockSpec(memory_space=pltpu.SMEM)
    hbm = pl.BlockSpec(memory_space=pltpu.HBM)
    residual, pixels = pl.pallas_call(
        kernel,
        out_shape=(
            jax.ShapeDtypeStruct((24, ROWS, NY), F32),
            jax.ShapeDtypeStruct((2, NY), F32),
        ),
        in_specs=[hbm, hbm, hbm, smem, hbm, hbm, hbm, hbm],
        out_specs=(vmem, vmem),
        scratch_shapes=[
            pltpu.VMEM((24, ROWS, NY), F32),
            pltpu.VMEM((3, ROWS, NY), F32),
            pltpu.VMEM((ROWS, NY), jnp.int32),
            pltpu.VMEM((24, 24), F32),
            pltpu.VMEM((384, 384), F32),
            pltpu.VMEM((1, NY), jnp.int32),
            pltpu.VMEM((3, 1, NY), F32),
            pltpu.VMEM((ROWS, 24, NY), F32),
            pltpu.VMEM((ROWS, 24, NY), F32),
            pltpu.VMEM((2, ROWS, 24, NY), F32),
            pltpu.VMEM((3, 2, 24, NY), F32),
            pltpu.VMEM((ROWS, NY), F32),
            pltpu.VMEM((3, ROWS, NY), F32),
            pltpu.VMEM((2, ROWS + 1, 1, NY), F32),
            pltpu.VMEM((3, 960, NY), BF16),
            pltpu.VMEM((ROWS + 1, 96, NY), F32),
            pltpu.VMEM((2, 192, 192), BF16),
            pltpu.VMEM((2, 2, 96, 192), BF16),
            pltpu.VMEM((ROWS, 24, NY), F32),
            pltpu.VMEM((ROWS, 32, NY), F32),
            pltpu.VMEM((2, 384, 384), BF16),
            pltpu.VMEM((8, NY), F32),
            pltpu.VMEM((8, NY), F32),
            pltpu.VMEM((NZ, 2, 1, 128), F32),
            pltpu.VMEM((NZ, 2, 1, 128), F32),
            pltpu.VMEM((7, 2, 1, 128), F32),
            pltpu.VMEM((2, NZ, 128), F32),
            pltpu.VMEM((8, NZ, 128), F32),
            pltpu.VMEM((2, SLABS, 128), F32),
            pltpu.VMEM((128, 128), F32),
            pltpu.VMEM((1, 128), F32),
            pltpu.VMEM((8, ND, 1, 128), F32),
            pltpu.VMEM((8, 1, 128), F32),
            pltpu.VMEM((NZ, 8, 1, 128), F32),
            pltpu.SemaphoreType.DMA((7,)),
            pltpu.SemaphoreType.DMA((92,)),
            pltpu.SemaphoreType.DMA((92,)),
        ],
        compiler_params=pltpu.CompilerParams(
            collective_id=0, has_side_effects=True, vmem_limit_bytes=60 * 1024 * 1024
        ),
    )(
        right_side.reshape(24, ROWS, NY),
        smoother.reshape(3, ROWS, NY),
        material.reshape(ROWS, NY),
        moduli,
        element_matrix,
        coarse_inverse,
        surface_map,
        line_of_sight,
    )
    return residual.reshape(right_side.shape), pixels


def solution(mesh):
    return jax.shard_map(
        body,
        mesh=mesh,
        in_specs=(
            P(None, None, "slab", "depth", None),
            P(None, "slab", "depth", None),
            P("slab", "depth", None),
            P(),
            P(),
            P(),
            P("slab", None),
            P(None, "slab", None),
        ),
        out_specs=(P(None, None, "slab", "depth", None), P("depth", "slab")),
        check_vma=False,
    )
```

```python
import jax
import jax.numpy as jnp
from jax import lax
from jax.experimental import pallas as pl
from jax.experimental.pallas import tpu as pltpu
from jax.sharding import PartitionSpec as P

F32, BF16 = jnp.float32, jnp.bfloat16
MESH = pl.DeviceIdType.MESH
HIGHEST = lax.Precision.HIGHEST
NX, NZ, NC, ND = 4, 16, 2, 4
SLABS, ROWS, NY = NX * NZ * NC, 8, 256
NODES = ROWS * ND * NY


def iota(shape, dim):
    return lax.broadcasted_iota(jnp.int32, shape, dim)


def dot(a, b):
    return jnp.dot(a, b, preferred_element_type=F32)


def dot_full(a, b):
    return jnp.dot(a, b, preferred_element_type=F32, precision=HIGHEST)


def dot_nt(a, b):
    return lax.dot_general(a, b, (((1,), (1,)), ((), ())), preferred_element_type=F32)


def split(v):
    high = v.astype(BF16)
    return high, (v - high.astype(F32)).astype(BF16)


def fsplit(v):
    high = v.astype(BF16).astype(F32)
    return high, v - high


def hot(mask):
    return jnp.where(mask, 1.0, 0.0).astype(F32)


def from_right(v):
    width = v.shape[1]
    return jnp.where(iota(v.shape, 1) == width - 1, 0.0, pltpu.roll(v, width - 1, axis=1))


def from_left(v):
    return jnp.where(iota(v.shape, 1) == 0, 0.0, pltpu.roll(v, 1, axis=1))


def to_row(columns):
    lane, sub = iota((8, 128), 1), iota((8, 128), 0)
    total = jnp.zeros((8, 128), F32)
    for q, column in enumerate(columns):
        total = jnp.where(lane == q * 8 + sub, column, total)
    return jnp.sum(total, axis=0, keepdims=True)


def pick_row(v, index):
    return jnp.sum(jnp.where(iota(v.shape, 0) == index, v, 0.0), axis=0, keepdims=True)


def kernel(
    r_hbm, s_hbm, mat_hbm, mod_ref, e_hbm, c_hbm, map_hbm, los_hbm,
    res_ref, pix_ref,
    r_ref, s_ref, mat_ref, e_ref, c_ref, map_ref, los_ref,
    rt, st, hp, hz, own_mod, mod_in, mods, w, f_own, lhs_own, lhs_nb, app, g_z,
    c_perm, pj_out, pj_in, px_out, px_raw, px_relay, px_mid, px_in, ordered, gps,
    y_out, y_in, z_out, all_in,
    load, send, recv,
):
    s, d = lax.axis_index("slab"), lax.axis_index("depth")
    x, z, c = s // 32, (s // 2) % 16, s % 2
    g = x * 2 + c
    half = g // 4
    up, down = lax.rem(s + 1, SLABS), lax.rem(s + SLABS - 1, SLABS)
    deeper, higher = lax.rem(d + 1, ND), lax.rem(d + ND - 1, ND)

    z_id = {j: lax.rem(z + j + NZ, NZ) for j in range(-8, 9)}
    z_steps = [1, 2, 3, 4, -1, -2, -3, -4]
    z_peer = {j: (x * 32 + z_id[j] * 2 + c, d) for j in z_steps}
    g_ids = [lax.rem(g + i, 8) for i in range(1, 8)]
    g_peers = [((i // 2) * 32 + z * 2 + i % 2, d) for i in g_ids]
    layer_peers = []
    for i in range(1, 32):
        h = lax.rem(g + i // ND, 8)
        layer_peers.append(((h // 2) * 32 + z * 2 + h % 2, lax.rem(d + i % ND, ND)))
    near = [(up, d), (down, d)] + [(a, b) for a in (up, down) for b in (deeper, higher)]

    barrier = pltpu.get_barrier_semaphore()
    peers = list(z_peer.values()) + near + layer_peers
    for peer in peers:
        pl.semaphore_signal(barrier, inc=1, device_id=peer, device_id_type=MESH)

    pairs = [
        (r_hbm, r_ref), (s_hbm, s_ref), (mat_hbm, mat_ref), (los_hbm, los_ref),
        (map_hbm, map_ref), (e_hbm, e_ref), (c_hbm, c_ref),
    ]
    loads = [pltpu.make_async_copy(a, b, load.at[i]) for i, (a, b) in enumerate(pairs)]
    for each in loads:
        each.start()

    def copy(src, dst, index, peer):
        return pltpu.make_async_remote_copy(
            src_ref=src, dst_ref=dst, send_sem=send.at[index], recv_sem=recv.at[index],
            device_id=peer, device_id_type=MESH,
        )

    loads[0].wait()
    loads[1].wait()
    field = jnp.transpose(r_ref[...], (1, 0, 2))
    rt[...] = field
    for k in range(ROWS):
        weight = jnp.concatenate(
            [jnp.broadcast_to(s_ref[m, k : k + 1, :], (8, NY)) for m in range(3)], axis=0
        )
        st[k] = field[k] * weight
    loads[2].wait()
    material = mat_ref[...]
    modulus = jnp.zeros((ROWS, NY), F32)
    for i in range(16):
        modulus = jnp.where(material == i, mod_ref[i], modulus)
    own_mod[...] = modulus
    loads[3].wait()
    shown = jnp.zeros((8, NY), F32)
    for m in range(3):
        shown = shown + los_ref[m] * st[ROWS - 1, m * 8 : m * 8 + 8, :]
    pj_out[...] = shown

    pl.semaphore_wait(barrier, len(peers))

    def shows():
        return [copy(pj_out, pj_in, 6 + i, (s, i)) for i in range(ND - 1)]

    @pl.when(d == ND - 1)
    def _():
        for each in shows():
            each.start()
        pj_in[...] = shown

    started = []
    for i, peer in enumerate([(down, d), (s, higher), (down, higher)]):
        started.append(copy(own_mod, mod_in.at[i], 3 + i, peer))
        started[-1].start()
    sides = []
    for plane, a in ((1, s), (2, down), (0, up)):
        sides.append((st.at[0], hz.at[plane, 1], (a, higher)))
        sides.append((st.at[ROWS - 1], hz.at[plane, 0], (a, deeper)))
    for i, (src, dst, peer) in enumerate(sides):
        started.append(copy(src, dst, 9 + i, peer))
        started[-1].start()
    for i, (plane, peer) in enumerate(((1, (down, d)), (0, (up, d)))):
        started.append(copy(st, hp.at[plane], 15 + i, peer))
        started[-1].start()

    block_sum = jnp.zeros((24, NY), F32)
    force_sum = jnp.zeros((24, NY), F32)
    for k in range(ROWS):
        block_sum = block_sum + rt[k]
        force_sum = force_sum + rt[k] * st[k]
    block_sum = jnp.sum(block_sum, axis=1, keepdims=True)
    force_sum = jnp.sum(force_sum, axis=1, keepdims=True)

    loads[5].wait()
    e = e_ref[...]
    rho, eps = iota((192, 24), 0), iota((192, 24), 1)
    picked = dot_full(hot(eps == (rho % 96) // 8 + 12 * (1 - rho // 96)), e)
    eps, kap = iota((24, 192), 0), iota((24, 192), 1)
    column = 6 * (kap // 96) + (kap % 48) // 8
    wide = [dot_full(picked, hot(eps == column + 12 * a)) for a in range(2)]
    rho, kap = iota((96, 192), 0), iota((96, 192), 1)
    same_source = rho % 8 == kap % 8
    first = same_source & (kap % 96 < 48)
    parts = [wide[1][:96], wide[0][96:], wide[0][:96], wide[1][96:]]
    for i, part in enumerate(parts):
        high, low = fsplit(part)
        high = jnp.where(same_source, high, 0.0).astype(BF16)
        low = jnp.where(first, low, 0.0).astype(BF16)
        if i < 2:
            lhs_own[0, i * 96 : i * 96 + 96] = high
            lhs_own[1, i * 96 : i * 96 + 96] = low
        else:
            lhs_nb[i - 2, 0] = high
            lhs_nb[i - 2, 1] = low

    loads[4].wait()
    target = map_ref[...]
    tile, in_tile = target >> 8, target & 255
    tile_col = jnp.transpose(jnp.broadcast_to(tile.astype(F32), (8, NY)))[:, 0:1]
    same = (tile_col == tile.astype(F32)) & (iota((NY, NY), 0) < iota((NY, NY), 1))
    rank = jnp.sum(hot(same), axis=0, keepdims=True).astype(jnp.int32)
    tile_g = (tile >> 5) * 2 + (tile & 1)
    place_row = (tile_g >> 2) * 16 + ((tile >> 1) & 15)
    place_lane = (tile_g & 3) * 32 + rank
    row_hot = hot(iota((32, NY), 0) == place_row)

    far = [5, 6, 7, 8, -5, -6, -7]

    @pl.when(d != ND - 1)
    def _():
        copy(pj_out, pj_in, 6 + d, (s, d)).wait_recv()

    shown = pj_in[...]
    values = [pick_row(shown, 2 * d), pick_row(shown, 2 * d + 1)]
    values += [los_ref[m] for m in range(3)] + [in_tile.astype(F32)]
    packed = jnp.zeros((64, 128), F32)
    for v, value in enumerate(values):
        high, low = fsplit(value)
        left = jnp.concatenate([row_hot * high, row_hot * low], axis=0).astype(BF16)
        right = hot(iota((128, NY), 0) == place_lane + 4 * v).astype(BF16)
        packed = packed + dot_nt(left, right)
    packed = packed[:32] + packed[32:]
    px_out[:, 0] = packed[:16].reshape(16, 1, 128)
    px_out[:, 1] = packed[16:].reshape(16, 1, 128)
    px_raw[z] = px_out[z]
    for i, j in enumerate(z_steps):
        started.append(copy(px_out.at[z_id[j]], px_raw.at[z], 17 + i, z_peer[j]))
        started[-1].start()
    for i, j in enumerate(far):
        peer = z_peer[4 if j > 0 else -4]
        started.append(copy(px_out.at[z_id[j]], px_relay.at[i], 25 + i, peer))
        started[-1].start()

    def weave(plane, index, value, alive):
        if alive is not None:
            value = jnp.where(alive, value, 0.0)
        high, low = split(jnp.concatenate([from_left(value), value], axis=0))
        w[plane, index * 96 : index * 96 + 48] = high
        w[plane, index * 96 + 48 : index * 96 + 96] = low

    for k in range(ROWS):
        weave(1, k + 1, st[k], None)

    for i in range(3):
        copy(own_mod, mod_in.at[i], 3 + i, (down, d)).wait_recv()
    inner = d < ND - 1
    last = s == SLABS - 1
    for k in range(ROWS):
        mods[0, k] = own_mod[k : k + 1, :]
        mods[1, k] = jnp.where(last, 0.0, mod_in[0, k : k + 1, :])
    mods[0, ROWS] = jnp.where(inner, mod_in[1, 0:1, :], 0.0)
    mods[1, ROWS] = jnp.where(inner & jnp.logical_not(last), mod_in[2, 0:1, :], 0.0)

    rho, eps = iota((128, 24), 0), iota((128, 24), 1)
    corner, rest = rho // 32, rho % 32
    comp, plane, comp2 = rest // 9, (rest % 9) // 3, rest % 3
    left = jnp.zeros((128, 8), F32)
    for layer in range(2):
        rows = dot_full(hot((eps == 12 * (1 - layer) + 3 * corner + comp) & (rest < 27)), e)
        keep = (eps % 3 == comp2) & (eps // 12 == plane - layer)
        of, to = iota((24, 8), 0), iota((24, 8), 1)
        gather = hot((to // 4 == layer) & ((of % 12) // 3 == to % 4))
        left = left + dot_full(jnp.where(keep, rows, 0.0), gather)
    high, low = fsplit(left)
    left_high = jnp.concatenate([high, high], axis=1).astype(BF16)
    left_low = jnp.concatenate([low, jnp.zeros_like(low)], axis=1).astype(BF16)
    before = None
    unit_sum = jnp.zeros((32, NY), F32)
    for k in range(ROWS + 1):
        sub, lane = iota((8, NY), 0), iota((8, NY), 1)
        block = jnp.where(sub < 4, mods[0, k], mods[1, k])
        there = (sub % 2 == 1) | (lane > 0)
        if k == 0:
            there = there & ((sub % 4 >= 2) | (d > 0))
        block = jnp.where(there, block, 0.0)
        high, low = fsplit(block)
        block = jnp.concatenate([high, low], axis=0).astype(BF16)
        now = dot(left_high, block) + dot(left_low, block)
        if before is not None:
            both = before[64:] + now[:64]
            both = both[32:] + from_right(both[:32])
            g_z[k - 1] = both
            unit_sum = unit_sum + both
        before = now
    unit_sum = jnp.sum(unit_sum, axis=1, keepdims=True)

    for i in range(6):
        copy(st.at[0], hz.at[0, 0], 9 + i, (s, higher)).wait_recv()
    not_first, not_last = s > 0, s < SLABS - 1
    weave(1, 0, hz[1, 0], d > 0)
    weave(1, 9, hz[1, 1], inner)
    for k in range(ROWS + 1):
        block = w[1, 96 * k : 96 * k + 192]
        f = dot(lhs_own[0], block) + dot(lhs_own[1], block)
        f_own[k] = mods[0, k] * f[:96] + mods[1, k] * f[96:]

    for i in range(7):
        copy(px_out.at[0], px_relay.at[0], 25 + i, (down, d)).wait_recv()
    for i, j in enumerate(far):
        origin, peer = (z_id[-4], z_peer[j - 4]) if j > 0 else (z_id[4], z_peer[j + 4])
        started.append(copy(px_relay.at[i], px_raw.at[origin], 39 + i, peer))
        started[-1].start()

    for i in range(2):
        copy(st, hp.at[i], 15 + i, (down, d)).wait_recv()
    for plane, index, alive in ((0, 0, not_first), (2, 1, not_last)):
        weave(plane, 0, hz[plane, 0], alive & (d > 0))
        weave(plane, 9, hz[plane, 1], alive & inner)
        for k in range(ROWS):
            weave(plane, k + 1, hp[index, k], alive)
    before = None
    near_sum = jnp.zeros((24, NY), F32)
    cross_sum = jnp.zeros((24, NY), F32)
    for k in range(ROWS + 1):
        now = f_own[k]
        for i in range(2):
            block = w[2 * i, 96 * k : 96 * k + 192]
            now = now + mods[i, k] * (dot(lhs_nb[i, 0], block) + dot(lhs_nb[i, 1], block))
        if before is not None:
            both = before[48:] + now[:48]
            both = both[24:] + from_right(both[:24])
            app[k - 1] = both
            near_sum = near_sum + both * st[k - 1]
            cross_sum = cross_sum + both
        before = now
    near_sum = jnp.sum(near_sum, axis=1, keepdims=True)
    cross_sum = jnp.sum(cross_sum, axis=1, keepdims=True)

    def thirds(v):
        return [v[m * 8 : m * 8 + 8] for m in range(3)]

    row = to_row(
        thirds(block_sum)
        + [sum(thirds(force_sum)), sum(thirds(near_sum))]
        + thirds(cross_sum)
        + [unit_sum[i * 8 : i * 8 + 8] for i in range(4)]
    )
    y_out[...] = row
    y_in[g, d] = row
    for i, peer in enumerate(layer_peers):
        started.append(copy(y_out, y_in.at[g, d], 61 + i, peer))
        started[-1].start()

    for i in range(8):
        copy(px_out.at[0], px_raw.at[0], 17 + i, (down, d)).wait_recv()
    for i in range(7):
        copy(px_relay.at[0], px_raw.at[0], 39 + i, (down, d)).wait_recv()
    pairs = px_raw.reshape(2 * NZ, 128)
    for i in range(2):
        px_mid[i] = pairs[pl.ds(i, NZ, stride=2), :]
    for i, peer in enumerate(g_peers):
        started.append(copy(px_mid.at[g_ids[i] // 4], px_in.at[g], 32 + i, peer))
        started[-1].start()
    px_in[g] = px_mid[half]

    for i in range(31):
        copy(y_out, y_in.at[0, 0], 61 + i, (down, d)).wait_recv()
    rows = y_in[:, 0] + y_in[:, 1] + y_in[:, 2] + y_in[:, 3]
    z_out[...] = rows
    all_in[z] = rows
    for i, j in enumerate(z_steps):
        started.append(copy(z_out, all_in.at[z], 46 + i, z_peer[j]))
        started[-1].start()

    loads[6].wait()
    order = hot(iota((384, 384), 0) == 3 * (iota((384, 384), 1) % 128) + iota((384, 384), 1) // 128)
    order_t = hot(iota((384, 384), 1) == 3 * (iota((384, 384), 0) % 128) + iota((384, 384), 0) // 128)
    order, order_t = order.astype(BF16), order_t.astype(BF16)
    for i, part in enumerate(split(c_ref[...])):
        c_perm[i] = dot(order_t, dot(part, order).astype(BF16)).astype(BF16)

    for i in range(7):
        copy(px_mid.at[0], px_in.at[0], 32 + i, (down, d)).wait_recv()
    for i in range(8):
        ordered[0, pl.ds((i // 2) * 32 + i % 2, NZ, stride=2), :] = px_in[i]
    gps[...] = jnp.transpose(ordered[0])
    group = gps[pl.ds(pl.multiple_of((g % 4) * 32, 32), 32), :]
    ids = group[20:24].astype(jnp.int32)
    bins_right = jnp.concatenate(
        [hot(iota((256, 128), 0) == ids[j : j + 1]) for j in range(4)], axis=1
    ).astype(BF16)

    for i in range(8):
        copy(z_out, all_in.at[0], 46 + i, (down, d)).wait_recv()
    for i, j in enumerate([1, 2, 3, 4, -1, -2, -3]):
        block = all_in.at[z_id[j]]
        started.append(copy(block, block, 54 + i, z_peer[-4 if j > 0 else 4]))
        started[-1].start()
    for i in range(7):
        copy(z_out, all_in.at[0], 54 + i, (down, d)).wait_recv()

    gathered = all_in.reshape(SLABS, 128)
    for i in range(8):
        ordered[1, pl.ds((i // 2) * 32 + i % 2, NZ, stride=2), :] = gathered[pl.ds(i, NZ, stride=8), :]
    slabs = jnp.transpose(ordered[1])
    sums = [slabs[q * 8 : q * 8 + 8] for q in range(8)]
    means = jnp.concatenate(sums[:3], axis=1) * (1.0 / NODES)
    high, low = fsplit(means)
    both = jnp.concatenate([high, low], axis=0).astype(BF16)
    solved = dot(both, c_perm[0])
    corr = solved[:8] + solved[8:] + dot(both, c_perm[1])[:8]
    corr = [corr[:, m * 128 : m * 128 + 128] for m in range(3)]

    shifted = [[from_left(v) for v in corr], corr, [from_right(v) for v in corr]]
    numerator, denominator = sums[3], sums[4]
    for m in range(3):
        numerator = numerator + corr[m] * sums[m]
        part = 2.0 * sums[5 + m]
        for p in range(3):
            for m2 in range(3):
                i = 64 + m * 9 + p * 3 + m2
                part = part + slabs[i : i + 1] * shifted[p][m2]
        denominator = denominator + corr[m] * part
    step = jnp.sum(numerator, axis=1, keepdims=True) / jnp.sum(denominator, axis=1, keepdims=True)
    lane = iota((8, 128), 1)
    mine = [
        [jnp.sum(jnp.where(lane == s, v, 0.0), axis=1, keepdims=True) for v in shifted[p]]
        for p in range(3)
    ]
    steps = jnp.concatenate([step] * 3, axis=0)
    for k in range(ROWS):
        grown = []
        for m in range(3):
            total = app[k, m * 8 : m * 8 + 8]
            for p in range(3):
                for m2 in range(3):
                    i = m * 9 + p * 3 + m2
                    total = total + mine[p][m2] * g_z[k, i : i + 1]
            grown.append(total)
        app[k] = rt[k] - steps * jnp.concatenate(grown, axis=0)
    res_ref[...] = jnp.transpose(app[...], (1, 0, 2))

    found = []
    for v in range(2):
        value = group[4 * v : 4 * v + 4]
        for m in range(3):
            value = value + group[8 + 4 * m : 12 + 4 * m] * pick_row(corr[m], 2 * d + v)
        found.append(jnp.concatenate([value[j : j + 1] for j in range(4)], axis=1))
    sub = iota((8, 512), 0)
    parts = [fsplit(v) for v in found]
    left = jnp.where(sub == 0, parts[0][0], jnp.where(sub == 1, parts[1][0], 0.0))
    left = jnp.where(sub == 2, parts[0][1], jnp.where(sub == 3, parts[1][1], left))
    bins = dot_nt(left.astype(BF16), bins_right)
    wide_step = jnp.broadcast_to(step, (8, NY))
    for v in range(2):
        pix_ref[v : v + 1, :] = pick_row(wide_step, 2 * d + v) * (
            bins[v : v + 1] + bins[v + 2 : v + 3]
        )

    for each in started:
        each.wait_send()

    @pl.when(d == ND - 1)
    def _():
        for each in shows():
            each.wait_send()


def body(right_side, smoother, material, moduli, element_matrix, coarse_inverse, surface_map, line_of_sight):
    vmem = pl.BlockSpec(memory_space=pltpu.VMEM)
    smem = pl.BlockSpec(memory_space=pltpu.SMEM)
    hbm = pl.BlockSpec(memory_space=pltpu.HBM)
    residual, pixels = pl.pallas_call(
        kernel,
        out_shape=(
            jax.ShapeDtypeStruct((24, ROWS, NY), F32),
            jax.ShapeDtypeStruct((2, NY), F32),
        ),
        in_specs=[hbm, hbm, hbm, smem, hbm, hbm, hbm, hbm],
        out_specs=(vmem, vmem),
        scratch_shapes=[
            pltpu.VMEM((24, ROWS, NY), F32),
            pltpu.VMEM((3, ROWS, NY), F32),
            pltpu.VMEM((ROWS, NY), jnp.int32),
            pltpu.VMEM((24, 24), F32),
            pltpu.VMEM((384, 384), F32),
            pltpu.VMEM((1, NY), jnp.int32),
            pltpu.VMEM((3, 1, NY), F32),
            pltpu.VMEM((ROWS, 24, NY), F32),
            pltpu.VMEM((ROWS, 24, NY), F32),
            pltpu.VMEM((2, ROWS, 24, NY), F32),
            pltpu.VMEM((3, 2, 24, NY), F32),
            pltpu.VMEM((ROWS, NY), F32),
            pltpu.VMEM((3, ROWS, NY), F32),
            pltpu.VMEM((2, ROWS + 1, 1, NY), F32),
            pltpu.VMEM((3, 960, NY), BF16),
            pltpu.VMEM((ROWS + 1, 96, NY), F32),
            pltpu.VMEM((2, 192, 192), BF16),
            pltpu.VMEM((2, 2, 96, 192), BF16),
            pltpu.VMEM((ROWS, 24, NY), F32),
            pltpu.VMEM((ROWS, 32, NY), F32),
            pltpu.VMEM((2, 384, 384), BF16),
            pltpu.VMEM((8, NY), F32),
            pltpu.VMEM((8, NY), F32),
            pltpu.VMEM((NZ, 2, 1, 128), F32),
            pltpu.VMEM((NZ, 2, 1, 128), F32),
            pltpu.VMEM((7, 2, 1, 128), F32),
            pltpu.VMEM((2, NZ, 128), F32),
            pltpu.VMEM((8, NZ, 128), F32),
            pltpu.VMEM((2, SLABS, 128), F32),
            pltpu.VMEM((128, 128), F32),
            pltpu.VMEM((1, 128), F32),
            pltpu.VMEM((8, ND, 1, 128), F32),
            pltpu.VMEM((8, 1, 128), F32),
            pltpu.VMEM((NZ, 8, 1, 128), F32),
            pltpu.SemaphoreType.DMA((7,)),
            pltpu.SemaphoreType.DMA((92,)),
            pltpu.SemaphoreType.DMA((92,)),
        ],
        compiler_params=pltpu.CompilerParams(
            collective_id=0, has_side_effects=True, vmem_limit_bytes=60 * 1024 * 1024
        ),
    )(
        right_side.reshape(24, ROWS, NY),
        smoother.reshape(3, ROWS, NY),
        material.reshape(ROWS, NY),
        moduli,
        element_matrix,
        coarse_inverse,
        surface_map,
        line_of_sight,
    )
    return residual.reshape(right_side.shape), pixels


def solution(mesh):
    return jax.shard_map(
        body,
        mesh=mesh,
        in_specs=(
            P(None, None, "slab", "depth", None),
            P(None, "slab", "depth", None),
            P("slab", "depth", None),
            P(),
            P(),
            P(),
            P("slab", None),
            P(None, "slab", None),
        ),
        out_specs=(P(None, None, "slab", "depth", None), P("depth", "slab")),
        check_vma=False,
    )
```
